32 devices in a mesh: blk: 16 (over z, y, core), rep: 2 (over x).
Axes of the slice: x: 2, y: 2, z: 4, core: 2. Of those that a mesh axis runs over, the one named last changes fastest.
Arguments:
- image_embed: bfloat16 [16384, 1152], P(('rep', 'blk')), parts along dimension 0, may hold values from -6 to 6
- text_embed: bfloat16 [16384, 1152], P(('rep', 'blk')), parts along dimension 0, may hold values from -6 to 6
Outputs:
- image_grad: float32 [16384, 1152], P(('rep', 'blk')), parts along dimension 0
- text_grad: float32 [16384, 1152], P(('rep', 'blk')), parts along dimension 0
The draws below stay inside these ranges and needn't reach their ends.
There are 2 independent parts, one for each index of `rep`. The reference program is written for one: setup_inputs(seed, part) draws one part's arguments, and reference() takes and returns one part's arrays. A program takes and returns all parts, laid end to end along the dimension named above; each array names one. Nothing has to cross between parts.
All inputs are finite; a program needn't handle non-finite values.
Results may differ from the reference program's by a relative error of at most 0.002.
Values may be sent and summed in bfloat16 or wider, within the bound.
No kernel may reach another device: no remote copies, remote signals or barrier semaphores. Data moves between devices by JAX's collectives and lax.ppermute only.
A program may use at most 64 MiB of HBM per device.

```python
import math
import jax
import jax.numpy as jnp

D = 1152
ROWS = 512
STEPS = 4
BATCH = 8192
N_BLK = 16


def block_levels(own_key, dims, pieces, low, top_value):
    def one(position, blocks):
        heights = jax.random.uniform(jax.random.fold_in(jax.random.fold_in(own_key, 6), position), (blocks,), jnp.float32, low / len(pieces), top_value / len(pieces))
        return jnp.repeat(jnp.exp(heights), dims[position] // blocks).reshape((-1,) + (1,) * (len(dims) - position - 1))

    loudness = one(*pieces[0])
    for cut in pieces[1:]:
        loudness = loudness * one(*cut)
    return loudness


def normal_values(rng, dims, width, most, pieces=(), held_as=jnp.bfloat16):
    values = width * jax.random.normal(rng, dims, jnp.float32)
    if pieces:
        values = values * block_levels(rng, dims, pieces, -0.22, 0.18)
    return jnp.clip(values, -most, most).astype(held_as)


def setup_inputs(seed: int = 0, part: int = 0) -> dict:
    keys = jax.random.split(jax.random.key(seed), 3)
    part_splits = jax.random.split(jax.random.fold_in(keys[2], part), 3)
    image_embed = normal_values(part_splits[0], (BATCH, D), 1.0, 6.0, ((0, 16),))
    text_embed = normal_values(part_splits[1], (BATCH, D), 1.0, 6.0, ((0, 16),))
    return dict(image_embed=image_embed, text_embed=text_embed)


def reference(image_embed, text_embed):
    factor = 2.0 / math.sqrt(D)
    img_blocks = image_embed.reshape(N_BLK, ROWS, D).astype(jnp.float32)
    txt_blocks = text_embed.reshape(N_BLK, ROWS, D).astype(jnp.float32)
    matched = jnp.eye(ROWS, dtype=jnp.float32)
    image_grad = jnp.zeros((N_BLK, ROWS, D), jnp.float32)
    text_grad = jnp.zeros((N_BLK, ROWS, D), jnp.float32)
    for offset in range(STEPS):
        visitor = jnp.roll(txt_blocks, offset, axis=0)
        inner_prod = jnp.einsum('kid,kjd->kij', img_blocks, visitor)
        chances = jax.nn.sigmoid(factor * inner_prod - 1.0)
        if offset == 0:
            chances = chances - matched
        weight = chances.astype(jnp.bfloat16).astype(jnp.float32)
        image_grad = image_grad + factor * jnp.einsum('kij,kjd->kid', weight, visitor)
        partial_value = factor * jnp.einsum('kij,kid->kjd', weight, img_blocks)
        text_grad = text_grad + jnp.roll(partial_value, -offset, axis=0)
    return (image_grad.reshape(BATCH, D), text_grad.reshape(BATCH, D))
```

```python
import math

import jax
import jax.numpy as jnp
from jax import lax
from jax.sharding import PartitionSpec as P

STEPS = 4
AXIS = "blk"


def send(block, target):
    count = lax.axis_size(AXIS)
    return lax.ppermute(block, AXIS, [(i, target(i) % count) for i in range(count)])


def weights(images, texts):
    factor = 2.0 / math.sqrt(images.shape[1])
    inner_prod = lax.dot_general(
        images, texts, (((1,), (1,)), ((), ())), preferred_element_type=jnp.float32
    )
    return jax.nn.sigmoid(factor * inner_prod - 1.0)


def image_term(weight, texts):
    return jnp.dot(weight, texts, preferred_element_type=jnp.float32)


def text_term(weight, images):
    return lax.dot_general(
        weight, images, (((0,), (0,)), ((), ())), preferred_element_type=jnp.float32
    )


def local(image_embed, text_embed):
    factor = 2.0 / math.sqrt(image_embed.shape[1])
    rows = image_embed.shape[0]

    text_2 = send(text_embed, lambda i: i + 2)
    image_2 = send(image_embed, lambda i: i - 2)
    text_x = send(text_embed, lambda i: i + 3 if i % 2 else i + 1)
    image_x = send(image_embed, lambda i: i - 1 if i % 2 else i - 3)
    text_s = send(text_2, lambda i: i ^ 1)
    image_s = send(image_2, lambda i: i ^ 1)

    row_ids = jnp.arange(rows)
    matched = (row_ids[:, None] == row_ids[None, :]).astype(jnp.float32)
    own = (weights(image_embed, text_embed) - matched).astype(jnp.bfloat16)
    image_grad = image_term(own, text_embed)
    text_grad = text_term(own, image_embed)
    for texts in (text_x, text_2, text_s):
        weight = weights(image_embed, texts).astype(jnp.bfloat16)
        image_grad = image_grad + image_term(weight, texts)
    for images in (image_x, image_2, image_s):
        weight = weights(images, text_embed).astype(jnp.bfloat16)
        text_grad = text_grad + text_term(weight, images)
    return (factor * image_grad, factor * text_grad)


def solution(mesh):
    spec = P(("rep", "blk"), None)
    return jax.shard_map(
        local, mesh=mesh, in_specs=(spec, spec), out_specs=(spec, spec), check_vma=False
    )
```

```python
import functools
import math

import jax
import jax.numpy as jnp
from jax import lax
from jax.experimental import pallas as pl
from jax.experimental.pallas import tpu as pltpu
from jax.sharding import PartitionSpec as P

AXIS = "blk"
SHARES = (8, 6, 2)
VMEM_MIB = 24
VMEM = pl.BlockSpec(memory_space=pltpu.VMEM)


def send(block, target):
    count = lax.axis_size(AXIS)
    return lax.ppermute(block, AXIS, [(i, target(i) % count) for i in range(count)])


def cut(block):
    rows = block.shape[0]
    ends = [0]
    for share in SHARES:
        ends.append(ends[-1] + rows * share // sum(SHARES))
    return [block[a:b] for a, b in zip(ends, ends[1:])]


def weights(rows, others, factor):
    inner_prod = lax.dot_general(
        rows, others, (((1,), (1,)), ((), ())), preferred_element_type=jnp.float32
    )
    return jax.nn.sigmoid(factor * inner_prod - 1.0)


def product(weight, others):
    return jnp.dot(weight.astype(jnp.bfloat16), others, preferred_element_type=jnp.float32)


def own_kernel(factor, image_ref, text_ref, image_out, text_out):
    images, texts = image_ref[...], text_ref[...]
    shape = (images.shape[0], texts.shape[0])
    matched = lax.broadcasted_iota(jnp.int32, shape, 0) == lax.broadcasted_iota(
        jnp.int32, shape, 1
    )
    matched = matched.astype(jnp.float32)
    image_out[...] = product(weights(images, texts, factor) - matched, texts)
    text_out[...] = product(weights(texts, images, factor) - matched, images)


def window_kernel(factor, n, image_ref, text_ref, *refs):
    texts, images = refs[:n], refs[n : 2 * n]
    image_sum, text_sum, image_out, text_out = refs[2 * n :]
    for own, others, total, out in (
        (image_ref, texts, image_sum, image_out),
        (text_ref, images, text_sum, text_out),
    ):
        rows = own[...]
        result = total[...]
        for other in others:
            block = other[...]
            result = result + product(weights(rows, block, factor), block)
        out[...] = result


def last_kernel(factor, tile, image_ref, text_ref, texts, images, *refs):
    image_sum, text_sum, image_out, text_out, held, sems = refs
    copies = []
    for own, other, total, out in (
        (image_ref, texts, image_sum, image_out),
        (text_ref, images, text_sum, text_out),
    ):
        block = other[...]
        for start in range(0, own.shape[0], tile):
            span = pl.ds(start, tile)
            result = total[span] + product(weights(own[span], block, factor), block)
            slot = len(copies)
            held[slot] = result * factor
            copies.append(pltpu.make_async_copy(held.at[slot], out.at[span], sems.at[slot]))
            copies[-1].start()
    for copy in copies:
        copy.wait()


def params():
    return pltpu.CompilerParams(vmem_limit_bytes=VMEM_MIB << 20)


def local(image_embed, text_embed):
    rows, width = image_embed.shape
    factor = 2.0 / math.sqrt(width)
    shape = (rows, width)
    kept = (pltpu.VMEM(shape, jnp.float32), pltpu.VMEM(shape, jnp.float32))

    def cost(visitors):
        return pl.CostEstimate(
            flops=8 * rows * width * visitors,
            bytes_accessed=8 * (rows + visitors) * width,
            transcendentals=4 * rows * visitors,
        )

    def start():
        return pl.pallas_call(
            functools.partial(own_kernel, factor),
            out_shape=kept,
            in_specs=[VMEM] * 2,
            out_specs=(VMEM, VMEM),
            cost_estimate=cost(rows),
            compiler_params=params(),
        )(image_embed, text_embed)

    def add(sums, texts, images):
        operands = (image_embed, text_embed, *texts, *images, *sums)
        n = len(operands)
        return pl.pallas_call(
            functools.partial(window_kernel, factor, len(texts)),
            out_shape=kept,
            in_specs=[VMEM] * n,
            out_specs=(VMEM, VMEM),
            input_output_aliases={n - 2: 0, n - 1: 1},
            cost_estimate=cost(sum(t.shape[0] for t in texts)),
            compiler_params=params(),
        )(*operands)

    def finish(sums, texts, images):
        tile = rows // 2
        return pl.pallas_call(
            functools.partial(last_kernel, factor, tile),
            out_shape=(jax.ShapeDtypeStruct(shape, jnp.float32),) * 2,
            in_specs=[VMEM] * 6,
            out_specs=(pl.BlockSpec(memory_space=pl.ANY),) * 2,
            scratch_shapes=[
                pltpu.VMEM((2 * rows // tile, tile, width), jnp.float32),
                pltpu.SemaphoreType.DMA((2 * rows // tile,)),
            ],
            cost_estimate=cost(texts.shape[0]),
            compiler_params=params(),
        )(image_embed, text_embed, texts, images, *sums)

    image_parts, text_parts = cut(image_embed), cut(text_embed)
    last = len(SHARES) - 1
    sums = start()
    parts = (text_parts[0], image_parts[0], text_parts[0], image_parts[0])
    targets = (
        lambda i: i + 2,
        lambda i: i - 2,
        lambda i: i + 3 if i % 2 else i + 1,
        lambda i: i - 1 if i % 2 else i - 3,
    )
    for k in range(last + 1):
        following = (text_parts[k + 1], image_parts[k + 1]) * 2 if k < last else parts
        arrived, gated = [], []
        for part, target, later in zip(parts, targets, following):
            piece, later, sums = lax.optimization_barrier((send(part, target), later, sums))
            arrived.append(piece)
            gated.append(later)
        parts = gated
        text_2, image_2, text_x, image_x = arrived
        text_s = send(text_2, lambda i: i ^ 1)
        image_s = send(image_2, lambda i: i ^ 1)
        if k == last:
            sums = add(sums, (text_2, text_x), (image_2, image_x))
            return tuple(finish(sums, text_s, image_s))
        sums = add(sums, (text_2, text_x, text_s), (image_2, image_x, image_s))


def solution(mesh):
    spec = P(("rep", "blk"), None)
    return jax.shard_map(
        local, mesh=mesh, in_specs=(spec, spec), out_specs=(spec, spec), check_vma=False
    )
```

```python
import functools
import math

import jax
import jax.numpy as jnp
from jax import lax
from jax.experimental import pallas as pl
from jax.experimental.pallas import tpu as pltpu
from jax.sharding import PartitionSpec as P

AXIS = "blk"
IMAGE_SHARES = (9, 16, 7)
TEXT_SHARES = (13, 12, 7)
DEPTH = 256
TILE = 256
VMEM_MIB = 28
VMEM = pl.BlockSpec(memory_space=pltpu.VMEM)
ANY = pl.BlockSpec(memory_space=pl.ANY)


def send(block, target):
    count = lax.axis_size(AXIS)
    return lax.ppermute(block, AXIS, [(i, target(i) % count) for i in range(count)])


def swap(block):
    return send(block, lambda i: i ^ 1)


def cut(block, shares):
    rows = block.shape[0]
    ends = [0]
    for share in shares:
        ends.append(ends[-1] + rows * share // sum(shares))
    return [block[a:b] for a, b in zip(ends, ends[1:])]


def after(value, *earlier):
    return lax.optimization_barrier((value, *earlier))[0]


def weights(rows, others, factor):
    inner_prod = lax.dot_general(
        rows, others, (((1,), (1,)), ((), ())), preferred_element_type=jnp.float32
    )
    return jax.nn.sigmoid(factor * inner_prod - 1.0)


def product(weight, others):
    return jnp.dot(weight.astype(jnp.bfloat16), others, preferred_element_type=jnp.float32)


def padded(rows):
    return -(-rows // DEPTH) * DEPTH


def join(visitors, joined):
    if len(visitors) == 1 and visitors[0].shape[0] % DEPTH == 0:
        return visitors[0]
    start = 0
    for visitor in visitors:
        joined[pl.ds(start, visitor.shape[0])] = visitor[...]
        start += visitor.shape[0]
    depth = padded(start)
    if start < depth:
        joined[pl.ds(start, depth - start)] = jnp.zeros(
            (depth - start, joined.shape[1]), joined.dtype
        )
    return joined.at[pl.ds(0, depth)]


def own_kernel(factor, image_ref, text_ref, image_out, text_out):
    for rows_ref, others_ref, out in (
        (image_ref, text_ref, image_out),
        (text_ref, image_ref, text_out),
    ):
        others = others_ref[...]
        for start in range(0, rows_ref.shape[0], TILE):
            span = pl.ds(start, TILE)
            shape = (TILE, others.shape[0])
            row = lax.broadcasted_iota(jnp.int32, shape, 0) + start
            matched = (row == lax.broadcasted_iota(jnp.int32, shape, 1)).astype(jnp.float32)
            weight = weights(rows_ref[span], others, factor) - matched
            out[span] = product(weight, others)


def window_kernel(factor, counts, *refs):
    refs = list(refs)
    sides = []
    for count in counts:
        sides.append((refs[0], refs[1 : 1 + count], refs[1 + count]))
        refs = refs[2 + count :]
    joined = refs[len(counts)]
    for (rows_ref, visitors, total), out in zip(sides, refs):
        others = join(visitors, joined)[...]
        for start in range(0, rows_ref.shape[0], TILE):
            span = pl.ds(start, TILE)
            weight = weights(rows_ref[span], others, factor)
            out[span] = total[span] + product(weight, others)


def last_kernel(factor, count, rows_ref, *refs):
    visitors, (total, out, joined, held, sems) = refs[:count], refs[count:]
    others = join(visitors, joined)[...]
    copies = []
    for start in range(0, rows_ref.shape[0], TILE):
        span = pl.ds(start, TILE)
        weight = weights(rows_ref[span], others, factor)
        held[span] = (total[span] + product(weight, others)) * factor
        copies.append(pltpu.make_async_copy(held.at[span], out.at[span], sems.at[len(copies)]))
        copies[-1].start()
    for copy in copies:
        copy.wait()


def params():
    return pltpu.CompilerParams(vmem_limit_bytes=VMEM_MIB << 20)


def local(image_embed, text_embed):
    rows, width = image_embed.shape
    factor = 2.0 / math.sqrt(width)
    shape = (rows, width)
    kept = pltpu.VMEM(shape, jnp.float32)

    cost = pl.CostEstimate(flops=1, bytes_accessed=1, transcendentals=0)

    def joined(sides):
        depth = max(padded(sum(v.shape[0] for v in visitors)) for visitors in sides)
        return pltpu.VMEM((depth, width), jnp.bfloat16)

    def begin():
        return pl.pallas_call(
            functools.partial(own_kernel, factor),
            out_shape=(kept, kept),
            in_specs=[VMEM] * 2,
            out_specs=(VMEM, VMEM),
            cost_estimate=cost,
            compiler_params=params(),
        )(image_embed, text_embed)

    def add(*sides):
        operands, aliases = [], {}
        for number, (own, visitors, total) in enumerate(sides):
            operands += [own, *visitors, total]
            aliases[len(operands) - 1] = number
        return pl.pallas_call(
            functools.partial(window_kernel, factor, [len(side[1]) for side in sides]),
            out_shape=(kept,) * len(sides),
            in_specs=[VMEM] * len(operands),
            out_specs=(VMEM,) * len(sides),
            scratch_shapes=[joined([side[1] for side in sides])],
            input_output_aliases=aliases,
            cost_estimate=cost,
            compiler_params=params(),
        )(*operands)

    def finish(own, visitors, total):
        return pl.pallas_call(
            functools.partial(last_kernel, factor, len(visitors)),
            out_shape=jax.ShapeDtypeStruct(shape, jnp.float32),
            in_specs=[VMEM] * (2 + len(visitors)),
            out_specs=ANY,
            scratch_shapes=[
                joined([visitors]),
                pltpu.VMEM(shape, jnp.float32),
                pltpu.SemaphoreType.DMA((rows // TILE,)),
            ],
            cost_estimate=cost,
            compiler_params=params(),
        )(own, *visitors, total)

    def next_text(piece):
        return send(piece, lambda i: i + 2)

    def next_image(piece):
        return send(piece, lambda i: i - 2)

    def far_text(piece):
        return send(piece, lambda i: i + 3 if i % 2 else i + 1)

    def far_image(piece):
        return send(piece, lambda i: i - 1 if i % 2 else i - 3)

    image_parts, text_parts = cut(image_embed, IMAGE_SHARES), cut(text_embed, TEXT_SHARES)
    text_x, image_x = far_text(text_embed), far_image(image_embed)
    text_piece, image_piece = next_text(text_parts[0]), next_image(image_parts[0])
    image_sum, text_sum = begin()

    image_0 = after(image_piece, image_sum, text_sum)
    image_piece = next_image(after(image_parts[1], image_0))
    image_0s = swap(image_0)
    (text_sum,) = add((text_embed, (image_0,), text_sum))

    text_0 = after(text_piece, text_sum)
    text_piece = next_text(after(text_parts[1], text_0))
    text_0s = swap(text_0)
    (image_sum,) = add((image_embed, (text_0,), image_sum))

    image_1 = after(image_piece, image_sum)
    image_piece = next_image(after(image_parts[2], image_1))
    image_1s = swap(image_1)
    (text_sum,) = add((text_embed, (image_1, image_0s), text_sum))

    text_1 = after(text_piece, text_sum)
    text_piece = next_text(after(text_parts[2], text_1))
    text_1s = swap(text_1)
    (image_sum,) = add((image_embed, (text_1, text_0s), image_sum))

    text_x, image_x = after(text_x, image_sum), after(image_x, image_sum)
    image_sum, text_sum = add(
        (image_embed, (text_x,), image_sum), (text_embed, (image_x,), text_sum)
    )

    image_2 = after(image_piece, image_sum)
    image_2s = swap(image_2)
    image_sum, text_sum = add(
        (image_embed, (text_1s,), image_sum), (text_embed, (image_2, image_1s), text_sum)
    )

    text_2 = after(text_piece, image_sum)
    text_2s = swap(text_2)
    text_grad = finish(text_embed, (after(image_2s, text_2),), text_sum)
    image_grad = finish(image_embed, (text_2, text_2s), image_sum)
    return (image_grad, text_grad)


def solution(mesh):
    spec = P(("rep", "blk"), None)
    return jax.shard_map(
        local, mesh=mesh, in_specs=(spec, spec), out_specs=(spec, spec), check_vma=False
    )
```

```python
import functools
import math

import jax
import jax.numpy as jnp
from jax import lax
from jax.experimental import pallas as pl
from jax.experimental.pallas import tpu as pltpu
from jax.sharding import PartitionSpec as P

AXIS = "blk"
TILE = 256
NEAR_PARTS = 2
VMEM_MIB = 32
VMEM = pl.BlockSpec(memory_space=pltpu.VMEM)
ANY = pl.BlockSpec(memory_space=pl.ANY)


def send(block, target):
    count = lax.axis_size(AXIS)
    return lax.ppermute(block, AXIS, [(i, target(i) % count) for i in range(count)])


def weights(rows, others, factor):
    inner_prod = lax.dot_general(
        rows, others, (((1,), (1,)), ((), ())), preferred_element_type=jnp.float32
    )
    return jax.nn.sigmoid(factor * inner_prod - 1.0)


def product(weight, others):
    return jnp.dot(weight.astype(jnp.bfloat16), others, preferred_element_type=jnp.float32)


def tiles(rows):
    return [pl.ds(start, TILE) for start in range(0, rows, TILE)]


def core():
    return lax.rem(lax.axis_index(AXIS), 2)


def pick_kernel(image_ref, text_ref, far_ref, near_ref, sems):
    def copy(far, near):
        copies = [
            pltpu.make_async_copy(far, far_ref, sems.at[0]),
            pltpu.make_async_copy(near, near_ref, sems.at[1]),
        ]
        for one in copies:
            one.start()
        for one in copies:
            one.wait()

    @pl.when(core() == 0)
    def _():
        copy(image_ref, text_ref)

    @pl.when(core() == 1)
    def _():
        copy(text_ref, image_ref)


def own_kernel(factor, image_ref, text_ref, near_own, *refs):
    near_parts, sums = refs[:NEAR_PARTS], refs[NEAR_PARTS]
    rows = image_ref.shape[0]
    for side, (own, others) in enumerate(((image_ref, text_ref), (text_ref, image_ref))):
        for span in tiles(rows):
            shape = (TILE, rows)
            row = lax.broadcasted_iota(jnp.int32, shape, 0) + span.start
            matched = (row == lax.broadcasted_iota(jnp.int32, shape, 1)).astype(jnp.float32)
            weight = weights(own[span], others[...], factor) - matched
            sums[side, span] = product(weight, others[...])
    side = 1 - core()
    for span in tiles(rows):
        for near_ref in near_parts:
            weight = weights(near_own[span], near_ref[...], factor)
            sums[side, span] += product(weight, near_ref[...])


def next_kernel(factor, image_ref, text_ref, texts, images, total, sums):
    for side, (own, others) in enumerate(((image_ref, texts), (text_ref, images))):
        for span in tiles(own.shape[0]):
            weight = weights(own[span], others[...], factor)
            sums[side, span] = total[side, span] + product(weight, others[...])


def last_kernel(factor, *refs):
    image_ref, text_ref, far_own, texts, images, far_ref, total = refs[:7]
    image_out, text_out, held, sems = refs[7:]
    rows = image_ref.shape[0]
    side = core()
    for span in tiles(rows):
        weight = weights(far_own[span], far_ref[...], factor)
        held[side, span] = total[side, span] + product(weight, far_ref[...])
        held[1 - side, span] = total[1 - side, span]
    copies = []
    for side, (own, others, out) in enumerate(
        ((image_ref, texts, image_out), (text_ref, images, text_out))
    ):
        for span in tiles(rows):
            weight = weights(own[span], others[...], factor)
            held[side, span] = (held[side, span] + product(weight, others[...])) * factor
            copy = pltpu.make_async_copy(held.at[side, span], out.at[span], sems.at[len(copies)])
            copy.start()
            copies.append(copy)
    for copy in copies:
        copy.wait()


def local(image_embed, text_embed):
    rows, width = image_embed.shape
    factor = 2.0 / math.sqrt(width)
    kept = pltpu.VMEM((2, rows, width), jnp.float32)
    block = pltpu.VMEM((rows, width), image_embed.dtype)
    cost = pl.CostEstimate(flops=1, bytes_accessed=1, transcendentals=0)
    params = pltpu.CompilerParams(vmem_limit_bytes=VMEM_MIB << 20)

    text_2 = send(text_embed, lambda i: i + 2)
    image_2 = send(image_embed, lambda i: i - 2)
    far_own, near_own = pl.pallas_call(
        pick_kernel,
        out_shape=(block, block),
        in_specs=[ANY, ANY],
        out_specs=(VMEM, VMEM),
        scratch_shapes=[pltpu.SemaphoreType.DMA((2,))],
        cost_estimate=cost,
        compiler_params=params,
    )(*(pltpu.with_memory_space_constraint(x, pltpu.HBM) for x in (image_embed, text_embed)))
    far = send(far_own, lambda i: i + 3 if i % 2 else i - 3)
    near = [send(part, lambda i: i ^ 1) for part in jnp.split(near_own, NEAR_PARTS)]
    sums = pl.pallas_call(
        functools.partial(own_kernel, factor),
        out_shape=kept,
        in_specs=[VMEM] * (3 + NEAR_PARTS),
        out_specs=VMEM,
        cost_estimate=cost,
        compiler_params=params,
    )(image_embed, text_embed, near_own, *near)
    text_2, image_2, sums = lax.optimization_barrier((text_2, image_2, sums))
    text_s = send(text_2, lambda i: i ^ 1)
    image_s = send(image_2, lambda i: i ^ 1)
    sums = pl.pallas_call(
        functools.partial(next_kernel, factor),
        out_shape=kept,
        in_specs=[VMEM] * 5,
        out_specs=VMEM,
        input_output_aliases={4: 0},
        cost_estimate=cost,
        compiler_params=params,
    )(image_embed, text_embed, text_2, image_2, sums)
    grad = jax.ShapeDtypeStruct((rows, width), jnp.float32)
    return pl.pallas_call(
        functools.partial(last_kernel, factor),
        out_shape=(grad, grad),
        in_specs=[VMEM] * 7,
        out_specs=(ANY, ANY),
        scratch_shapes=[
            pltpu.VMEM((2, rows, width), jnp.float32),
            pltpu.SemaphoreType.DMA((2 * rows // TILE,)),
        ],
        cost_estimate=cost,
        compiler_params=params,
    )(image_embed, text_embed, far_own, text_s, image_s, far, sums)


def solution(mesh):
    spec = P(("rep", "blk"), None)
    return jax.shard_map(
        local, mesh=mesh, in_specs=(spec, spec), out_specs=(spec, spec), check_vma=False
    )
```

```python
import functools
import math

import jax
import jax.numpy as jnp
from jax import lax
from jax.experimental import pallas as pl
from jax.experimental.pallas import tpu as pltpu
from jax.sharding import PartitionSpec as P

AXIS = "blk"
TILE = 256
NEAR_PARTS = 2
SWAP_PARTS = 2
VMEM_MIB = 32
VMEM = pl.BlockSpec(memory_space=pltpu.VMEM)
ANY = pl.BlockSpec(memory_space=pl.ANY)
LOG2_E = math.log2(math.e)


def send(block, target):
    count = lax.axis_size(AXIS)
    return lax.ppermute(block, AXIS, [(i, target(i) % count) for i in range(count)])


def swap(block):
    return [send(part, lambda i: i ^ 1) for part in jnp.split(block, SWAP_PARTS)]


def core():
    return lax.rem(lax.axis_index(AXIS), 2)


def tiles(rows):
    return [pl.ds(start, TILE) for start in range(0, rows, TILE)]


def logits(own, span, others):
    return lax.dot_general(
        own[span], others[...], (((1,), (1,)), ((), ())), preferred_element_type=jnp.float32
    )


def grow(factor, inner_prod):
    return jnp.exp2(LOG2_E - (factor * LOG2_E) * inner_prod)


def product(weight, others):
    return jnp.dot(weight.astype(jnp.bfloat16), others[...], preferred_element_type=jnp.float32)


def add_all(factor, units):
    following = logits(*units[0][:3])
    for k, (_, span, others, use) in enumerate(units):
        inner_prod = following
        if k + 1 < len(units):
            following = logits(*units[k + 1][:3])
        weight = pl.reciprocal(1.0 + grow(factor, inner_prod), approx=True)
        use(span, product(weight, others))


def join(visitors, joined):
    start = 0
    for visitor in visitors:
        joined[pl.ds(start, visitor.shape[0])] = visitor[...]
        start += visitor.shape[0]
    return joined


def pick_kernel(image_ref, text_ref, *refs):
    sides, sems = refs[:2], refs[2]

    def copy(*sources):
        copies = [
            pltpu.make_async_copy(source, side, sems.at[k])
            for k, (source, side) in enumerate(zip(sources, sides))
        ]
        for one in copies:
            one.start()
        for one in copies:
            one.wait()

    @pl.when(core() == 0)
    def _():
        copy(image_ref, text_ref)

    @pl.when(core() == 1)
    def _():
        copy(text_ref, image_ref)


def own_kernel(factor, side_0, side_1, *refs):
    near, (sum_0, sum_1, joined) = refs[:NEAR_PARTS], refs[NEAR_PARTS:]
    rows = side_0.shape[0]
    for own, others, total in ((side_0, side_1, sum_0), (side_1, side_0, sum_1)):
        for span in tiles(rows):
            shape = (TILE, rows)
            row = lax.broadcasted_iota(jnp.int32, shape, 0) + span.start
            matched = (row == lax.broadcasted_iota(jnp.int32, shape, 1)).astype(jnp.float32)
            weight = 1.0 / (1.0 + grow(factor, logits(own, span, others))) - matched
            total[span] = product(weight, others)

    def use(span, value):
        sum_1[span] += value

    others = join(near, joined)
    add_all(factor, [(side_1, span, others, use) for span in tiles(rows)])


def both_kernel(factor, side_0, side_1, visitor_0, *refs):
    visitors_1, (total_0, total_1, sum_0, sum_1, joined) = refs[:SWAP_PARTS], refs[SWAP_PARTS:]

    def use_0(span, value):
        sum_0[span] = total_0[span] + value

    def use_1(span, value):
        sum_1[span] = total_1[span] + value

    spans = tiles(side_0.shape[0])
    units = [(side_0, span, visitor_0, use_0) for span in spans]
    visitor_1 = join(visitors_1, joined)
    units += [(side_1, span, visitor_1, use_1) for span in spans]
    add_all(factor, units)


def one_kernel(factor, scale, own, visitor, total, out):
    def use(span, value):
        out[span] = (total[span] + value) * scale

    add_all(factor, [(own, span, visitor, use) for span in tiles(own.shape[0])])


def last_kernel(factor, side_0, *refs):
    visitors, refs = refs[:SWAP_PARTS], refs[SWAP_PARTS:]
    total, grad_1, image_out, text_out, held, joined, sems = refs
    spans = tiles(side_0.shape[0])

    def move(k, is_core):
        outs = (text_out, image_out) if is_core else (image_out, text_out)
        if k == len(spans):
            return pltpu.make_async_copy(grad_1, outs[1], sems.at[k])
        return pltpu.make_async_copy(held.at[spans[k]], outs[0].at[spans[k]], sems.at[k])

    def each(which, act):
        for is_core in (0, 1):

            @pl.when(core() == is_core)
            def _():
                for k in which:
                    act(move(k, is_core))

    def use(span, value):
        held[span] = (total[span] + value) * factor
        each((span.start // TILE,), lambda copy: copy.start())

    each((len(spans),), lambda copy: copy.start())
    visitor = join(visitors, joined)
    add_all(factor, [(side_0, span, visitor, use) for span in spans])
    each(range(len(spans) + 1), lambda copy: copy.wait())


def local(image_embed, text_embed):
    rows, width = image_embed.shape
    factor = 2.0 / math.sqrt(width)
    kept = pltpu.VMEM((rows, width), jnp.float32)
    block = pltpu.VMEM((rows, width), image_embed.dtype)
    grad = jax.ShapeDtypeStruct((rows, width), jnp.float32)

    def call(kernel, outs, operands, scratch=(), aliases=None, in_spec=VMEM, flops=1):
        spec = ANY if outs[0] is grad else VMEM
        return pl.pallas_call(
            kernel,
            out_shape=tuple(outs),
            in_specs=[in_spec] * len(operands),
            out_specs=(spec,) * len(outs),
            scratch_shapes=list(scratch),
            input_output_aliases=aliases or {},
            cost_estimate=pl.CostEstimate(flops=flops, bytes_accessed=1, transcendentals=0),
            compiler_params=pltpu.CompilerParams(vmem_limit_bytes=VMEM_MIB << 20),
        )(*operands)

    side_0, side_1 = call(
        pick_kernel,
        (block, block),
        [pltpu.with_memory_space_constraint(x, pltpu.HBM) for x in (image_embed, text_embed)],
        [pltpu.SemaphoreType.DMA((2,))],
        in_spec=ANY,
    )
    near = swap(side_1)
    ahead = send(side_1, lambda i: i - 2 if i % 2 else i + 2)
    far = send(side_0, lambda i: i + 3 if i % 2 else i - 3)
    sum_0, sum_1 = call(
        functools.partial(own_kernel, factor), (kept, kept), (side_0, side_1, *near), [block]
    )
    later, sum_0, sum_1 = lax.optimization_barrier((side_0, sum_0, sum_1))
    behind = send(later, lambda i: i + 2 if i % 2 else i - 2)

    ahead, sum_0, sum_1 = lax.optimization_barrier((ahead, sum_0, sum_1))
    sum_0, sum_1 = call(
        functools.partial(both_kernel, factor),
        (kept, kept),
        (side_0, side_1, ahead, *swap(ahead), sum_0, sum_1),
        [block],
        {3 + SWAP_PARTS: 0, 4 + SWAP_PARTS: 1},
    )
    far, sum_0 = lax.optimization_barrier((far, sum_0))
    (sum_0,) = call(
        functools.partial(one_kernel, factor, 1.0),
        (kept,),
        (side_0, far, sum_0),
        aliases={2: 0},
        flops=1 << 30,
    )
    behind, sum_0 = lax.optimization_barrier((behind, sum_0))
    (grad_1,) = call(
        functools.partial(one_kernel, factor, factor),
        (kept,),
        (side_1, behind, sum_1),
        aliases={2: 0},
    )
    return call(
        functools.partial(last_kernel, factor),
        (grad, grad),
        (side_0, *swap(behind), sum_0, grad_1),
        [kept, block, pltpu.SemaphoreType.DMA((rows // TILE + 1,))],
    )


def solution(mesh):
    spec = P(("rep", "blk"), None)
    return jax.shard_map(
        local, mesh=mesh, in_specs=(spec, spec), out_specs=(spec, spec), check_vma=False
    )
```

```python
import functools
import math

import jax
import jax.numpy as jnp
from jax import lax
from jax.experimental import pallas as pl
from jax.experimental.pallas import tpu as pltpu
from jax.sharding import PartitionSpec as P

AXIS = "blk"
TEXT_PARTS = 2
SWAP_PARTS = 4
NEAR_PARTS = 1
LAST_TILE = 256
COPY_ROWS = 128
VMEM_MIB = 32
VMEM = pl.BlockSpec(memory_space=pltpu.VMEM)
ANY = pl.BlockSpec(memory_space=pl.ANY)
LOG2_E = math.log2(math.e)


def send(block, target):
    count = lax.axis_size(AXIS)
    return lax.ppermute(block, AXIS, [(i, target(i) % count) for i in range(count)])


def swap(block, parts):
    return [send(part, lambda i: i ^ 1) for part in jnp.split(block, parts)]


def core():
    return lax.rem(lax.axis_index(AXIS), 2)


def logits(own, others):
    return lax.dot_general(
        own[...], others[...], (((1,), (1,)), ((), ())), preferred_element_type=jnp.float32
    )


def decay(factor, inner_prod):
    return jnp.exp2(LOG2_E - (factor * LOG2_E) * inner_prod)


def product(weight, others):
    return jnp.dot(weight.astype(jnp.bfloat16), others[...], preferred_element_type=jnp.float32)


def add_all(factor, units):
    following = logits(*units[0][:2])
    for k, (_, others, use) in enumerate(units):
        inner_prod = following
        if k + 1 < len(units):
            following = logits(*units[k + 1][:2])
        weight = pl.reciprocal(1.0 + decay(factor, inner_prod), approx=True)
        use(product(weight, others))


def join(visitors, joined):
    start = 0
    for visitor in visitors:
        joined[pl.ds(start, visitor.shape[0])] = visitor[...]
        start += visitor.shape[0]
    return joined


def pick_kernel(image_ref, text_ref, *refs):
    parts, (far_own, near_own, sems) = refs[:TEXT_PARTS], refs[TEXT_PARTS:]
    rows = parts[0].shape[0]
    for is_core, (far, near) in enumerate(((image_ref, text_ref), (text_ref, image_ref))):

        @pl.when(core() == is_core)
        def _():
            moves = [(text_ref.at[pl.ds(k * rows, rows)], part) for k, part in enumerate(parts)]
            moves += [(far, far_own), (near, near_own)]
            copies = [pltpu.make_async_copy(*move, sems.at[k]) for k, move in enumerate(moves)]
            for copy in copies:
                copy.start()
            for copy in copies:
                copy.wait()


def own_kernel(factor, image_ref, text_ref, image_sum, text_sum):
    rows = image_ref.shape[0]
    shape = (rows, rows)
    matched = lax.broadcasted_iota(jnp.int32, shape, 0) == lax.broadcasted_iota(
        jnp.int32, shape, 1
    )
    for own, others, total in ((image_ref, text_ref, image_sum), (text_ref, image_ref, text_sum)):
        chance = 1.0 / (1.0 + decay(factor, logits(own, others)))
        total[...] = product(chance - matched.astype(jnp.float32), others)


def text_kernel(factor, image_ref, near_own, *refs):
    near, refs = refs[:NEAR_PARTS], refs[NEAR_PARTS:]
    texts, refs = refs[:TEXT_PARTS], refs[TEXT_PARTS:]
    swapped, refs = refs[:SWAP_PARTS], refs[SWAP_PARTS:]
    image_total, text_total, image_sum, text_sum, *joined = refs
    is_1 = core().astype(jnp.float32)

    def use_near(value):
        image_sum[...] = image_total[...] + value * is_1
        text_sum[...] = text_total[...] + value * (1.0 - is_1)

    def use(value):
        image_sum[...] += value

    units = [(near_own, join(near, joined[0]), use_near)]
    units.append((image_ref, join(texts, joined[1]), use))
    units.append((image_ref, join(swapped, joined[2]), use))
    add_all(factor, units)


def image_kernel(factor, text_ref, images, text_total, text_sum):
    def use(value):
        text_sum[...] = text_total[...] + value

    add_all(factor, [(text_ref, images, use)])


def last_kernel(factor, text_ref, far_own, far, *refs):
    swapped, refs = refs[:SWAP_PARTS], refs[SWAP_PARTS:]
    image_total, text_total, image_out, text_out, image_held, text_held, joined, sems = refs
    rows = text_ref.shape[0]
    is_1 = core().astype(jnp.float32)
    copies = []

    def leave(held, out, start):
        for first in range(start, start + LAST_TILE, COPY_ROWS):
            span = pl.ds(first, COPY_ROWS)
            copies.append(pltpu.make_async_copy(held.at[span], out.at[span], sems.at[len(copies)]))
            copies[-1].start()

    def use_far(start):
        span = pl.ds(start, LAST_TILE)

        def use(value):
            image_held[span] = (image_total[span] + value * (1.0 - is_1)) * factor
            leave(image_held, image_out, start)
            text_held[span] = text_total[span] + value * is_1

        return (far_own.at[span], far, use)

    def use_swapped(start):
        span = pl.ds(start, LAST_TILE)

        def use(value):
            text_held[span] = (text_held[span] + value) * factor
            leave(text_held, text_out, start)

        return (text_ref.at[span], joined, use)

    join(swapped, joined)
    starts = range(0, rows, LAST_TILE)
    add_all(factor, [use_far(start) for start in starts] + [use_swapped(start) for start in starts])
    for copy in copies:
        copy.wait()


def local(image_embed, text_embed):
    rows, width = image_embed.shape
    factor = 2.0 / math.sqrt(width)
    kept = pltpu.VMEM((rows, width), jnp.float32)
    block = pltpu.VMEM((rows, width), image_embed.dtype)
    part = pltpu.VMEM((rows // TEXT_PARTS, width), image_embed.dtype)
    grad = jax.ShapeDtypeStruct((rows, width), jnp.float32)

    def call(kernel, outs, operands, scratch=(), aliases=None, in_spec=VMEM):
        return pl.pallas_call(
            kernel,
            out_shape=tuple(outs),
            in_specs=[in_spec] * len(operands),
            out_specs=(ANY if outs[0] is grad else VMEM,) * len(outs),
            scratch_shapes=list(scratch),
            input_output_aliases=aliases or {},
            cost_estimate=pl.CostEstimate(flops=1, bytes_accessed=1, transcendentals=0),
            compiler_params=pltpu.CompilerParams(vmem_limit_bytes=VMEM_MIB << 20),
        )(*operands)

    def after(values, earlier):
        out = lax.optimization_barrier((*values, *earlier))
        return out[: len(values)], out[len(values) :]

    *text_parts, far_own, near_own = call(
        pick_kernel,
        [part] * TEXT_PARTS + [block, block],
        [pltpu.with_memory_space_constraint(x, pltpu.HBM) for x in (image_embed, text_embed)],
        [pltpu.SemaphoreType.DMA((TEXT_PARTS + 2,))],
        in_spec=ANY,
    )
    texts = [send(piece, lambda i: i + 2) for piece in text_parts]
    images = send(image_embed, lambda i: i - 2)
    far = send(far_own, lambda i: i + 3 if i % 2 else i - 3)
    sums = call(functools.partial(own_kernel, factor), (kept, kept), (image_embed, text_embed))

    texts, sums = after(texts, sums)
    swapped = [part for text in texts for part in swap(text, SWAP_PARTS // TEXT_PARTS)]
    near = swap(near_own, NEAR_PARTS)
    count = 2 + NEAR_PARTS + TEXT_PARTS + SWAP_PARTS
    sums = call(
        functools.partial(text_kernel, factor),
        (kept, kept),
        (image_embed, near_own, *near, *texts, *swapped, *sums),
        [block] * 3,
        {count: 0, count + 1: 1},
    )
    (images,), (image_sum, text_sum) = after((images,), sums)
    swapped = swap(images, SWAP_PARTS)
    (text_sum,) = call(
        functools.partial(image_kernel, factor), (kept,), (text_embed, images, text_sum), (), {2: 0}
    )
    return call(
        functools.partial(last_kernel, factor),
        (grad, grad),
        (text_embed, far_own, far, *swapped, image_sum, text_sum),
        [kept, kept, block, pltpu.SemaphoreType.DMA((2 * rows // COPY_ROWS,))],
    )


def solution(mesh):
    spec = P(("rep", "blk"), None)
    return jax.shard_map(
        local, mesh=mesh, in_specs=(spec, spec), out_specs=(spec, spec), check_vma=False
    )
```

```python
import functools
import math

import jax
import jax.numpy as jnp
from jax import lax
from jax.experimental import pallas as pl
from jax.experimental.pallas import tpu as pltpu
from jax.sharding import PartitionSpec as P

AXIS = "blk"
FIRST_IMAGES = 8
FIRST_TEXTS = 10
LAST_TILE = 256
COPY_ROWS = 128
VMEM_MIB = 32
VMEM = pl.BlockSpec(memory_space=pltpu.VMEM)
ANY = pl.BlockSpec(memory_space=pl.ANY)
LOG2_E = math.log2(math.e)


def send(block, target, senders=(0, 1)):
    count = lax.axis_size(AXIS)
    route = [(i, target(i) % count) for i in range(count) if i % 2 in senders]
    return lax.ppermute(block, AXIS, route)


def swap(block, parts):
    return [send(part, lambda i: i ^ 1) for part in jnp.split(block, parts)]


def core():
    return lax.rem(lax.axis_index(AXIS), 2)


def logits(own, others):
    return lax.dot_general(
        own[...], others[...], (((1,), (1,)), ((), ())), preferred_element_type=jnp.float32
    )


def decay(factor, inner_prod):
    return jnp.exp2(LOG2_E - (factor * LOG2_E) * inner_prod)


def product(weight, others):
    return jnp.dot(weight.astype(jnp.bfloat16), others[...], preferred_element_type=jnp.float32)


def add_all(factor, units):
    following = logits(*units[0][:2])
    for k, (_, others, use) in enumerate(units):
        inner_prod = following
        if k + 1 < len(units):
            following = logits(*units[k + 1][:2])
        weight = pl.reciprocal(1.0 + decay(factor, inner_prod), approx=True)
        use(product(weight, others))


def join(visitors, joined):
    if len(visitors) == 1:
        return visitors[0]
    start = 0
    for visitor in visitors:
        joined[pl.ds(start, visitor.shape[0])] = visitor[...]
        start += visitor.shape[0]
    return joined.at[pl.ds(0, start)]


def pick_kernel(image_ref, text_ref, *refs):
    outs, sems = refs[:2], refs[2]
    copies = []
    for k, (source, out) in enumerate(zip((image_ref, text_ref), outs)):
        rows = pl.ds(0, out.shape[0])
        copies.append(pltpu.make_async_copy(source.at[rows], out, sems.at[k]))
        copies[-1].start()
    for copy in copies:
        copy.wait()


def core_pick_kernel(image_ref, text_ref, far_own, sem):
    for is_core, far in enumerate((image_ref, text_ref)):

        @pl.when(core() == is_core)
        def _():
            copy = pltpu.make_async_copy(far, far_own, sem)
            copy.start()
            copy.wait()


def own_kernel(factor, image_ref, text_ref, image_sum, text_sum):
    rows = image_ref.shape[0]
    shape = (rows, rows)
    matched = lax.broadcasted_iota(jnp.int32, shape, 0) == lax.broadcasted_iota(
        jnp.int32, shape, 1
    )
    for own, others, total in ((image_ref, text_ref, image_sum), (text_ref, image_ref, text_sum)):
        chance = 1.0 / (1.0 + decay(factor, logits(own, others)))
        total[...] = product(chance - matched.astype(jnp.float32), others)


def step_kernel(factor, units, sides, *refs):
    is_1 = core().astype(jnp.float32)
    parts = []
    for _, count in units:
        parts.append((refs[0], refs[1 : 1 + count]))
        refs = refs[1 + count :]
    totals = dict(zip(sides, refs))
    sums = dict(zip(sides, refs[len(sides) :]))
    joined = refs[2 * len(sides) :]
    touched = set()

    def add(side, value):
        sums[side][...] = (sums if side in touched else totals)[side][...] + value
        touched.add(side)

    def use(side, value):
        if side < 2:
            add(side, value)
        else:
            add(side - 2, value * (1.0 - is_1))
            add(3 - side, value * is_1)

    add_all(
        factor,
        [
            (own, join(visitors, scratch), functools.partial(use, side))
            for (side, _), (own, visitors), scratch in zip(units, parts, joined)
        ],
    )


def last_kernel(factor, counts, *refs):
    parts = []
    for count in counts:
        parts.append((refs[0], refs[1 : 1 + count], refs[1 + count]))
        refs = refs[2 + count :]
    outs, helds, joined, sems = refs[:2], refs[2:4], refs[4:6], refs[6]
    copies = []

    def use(total, held, out, start, value):
        rows = pl.ds(start, LAST_TILE)
        held[rows] = (total[rows] + value) * factor
        for first in range(start, start + LAST_TILE, COPY_ROWS):
            span = pl.ds(first, COPY_ROWS)
            copies.append(pltpu.make_async_copy(held.at[span], out.at[span], sems.at[len(copies)]))
            copies[-1].start()

    units = []
    for (own, visitors, total), held, out, scratch in zip(parts, helds, outs, joined):
        others = join(visitors, scratch)
        for start in range(0, own.shape[0], LAST_TILE):
            act = functools.partial(use, total, held, out, start)
            units.append((own.at[pl.ds(start, LAST_TILE)], others, act))
    add_all(factor, units)
    for copy in copies:
        copy.wait()


def local(image_embed, text_embed):
    rows, width = image_embed.shape
    dtype = image_embed.dtype
    factor = 2.0 / math.sqrt(width)
    kept = pltpu.VMEM((rows, width), jnp.float32)
    block = pltpu.VMEM((rows, width), dtype)
    grad = jax.ShapeDtypeStruct((rows, width), jnp.float32)

    def call(kernel, outs, operands, scratch=(), aliases=None, in_spec=VMEM):
        return pl.pallas_call(
            kernel,
            out_shape=tuple(outs),
            in_specs=[in_spec] * len(operands),
            out_specs=(ANY if outs[0] is grad else VMEM,) * len(outs),
            scratch_shapes=list(scratch),
            input_output_aliases=aliases or {},
            cost_estimate=pl.CostEstimate(flops=1, bytes_accessed=1, transcendentals=0),
            compiler_params=pltpu.CompilerParams(vmem_limit_bytes=VMEM_MIB << 20),
        )(*operands)

    def depth(visitors):
        return pltpu.VMEM((sum(visitor.shape[0] for visitor in visitors), width), dtype)

    def step(units, sums):
        sides = tuple(sums)
        operands = [ref for _, own, visitors in units for ref in (own, *visitors)]
        counts = [(side, len(visitors)) for side, _, visitors in units]
        return dict(
            zip(
                sides,
                call(
                    functools.partial(step_kernel, factor, counts, sides),
                    [kept] * len(sides),
                    (*operands, *sums.values()),
                    [depth(visitors) for _, _, visitors in units],
                    {len(operands) + k: k for k in range(len(sides))},
                ),
            )
        )

    def after(value, *earlier):
        return lax.optimization_barrier((value, *earlier))[0]

    def next_images(piece):
        return send(piece, lambda i: i - 2)

    def next_texts(piece):
        return send(piece, lambda i: i + 2)

    in_hbm = [pltpu.with_memory_space_constraint(x, pltpu.HBM) for x in (image_embed, text_embed)]
    cut_images, cut_texts = rows * FIRST_IMAGES // 16, rows * FIRST_TEXTS // 16
    heads = (cut_images, cut_texts)
    image_head, text_head = call(
        pick_kernel,
        [pltpu.VMEM((head, width), dtype) for head in heads],
        in_hbm,
        [pltpu.SemaphoreType.DMA((2,))],
        in_spec=ANY,
    )
    images, texts = next_images(image_head), next_texts(text_head)
    (far_own,) = call(
        core_pick_kernel, [block], in_hbm, [pltpu.SemaphoreType.DMA], in_spec=ANY
    )
    far = send(far_own, lambda i: i + 3 if i % 2 else i - 3)
    near_text = send(text_embed, lambda i: i + 1, (0,))
    near_image = send(image_embed, lambda i: i - 1, (1,))
    sums = call(functools.partial(own_kernel, factor), (kept, kept), (image_embed, text_embed))
    sums = step(
        [(0, image_embed, (near_text,)), (1, text_embed, (near_image,))],
        dict(enumerate(sums)),
    )

    images = after(images, *sums.values())
    later_images = next_images(after(image_embed[cut_images:], images))
    sums |= step([(1, text_embed, (images, *swap(images, 2)))], {1: sums[1]})
    texts = after(texts, *sums.values())
    later_texts = next_texts(after(text_embed[cut_texts:], texts))
    sums |= step([(0, image_embed, (texts, *swap(texts, 2)))], {0: sums[0]})
    sums = step([(2, far_own, (after(far, sums[0]),))], sums)

    images, texts = after(later_images, sums[0]), after(later_texts, sums[0])
    swapped_images, swapped_texts = swap(images, 2), swap(texts, 1)
    sums = step([(1, text_embed, (images,)), (0, image_embed, (texts,))], sums)
    operands = (image_embed, *swapped_texts, sums[0], text_embed, *swapped_images, sums[1])
    return call(
        functools.partial(last_kernel, factor, (1, 2)),
        (grad, grad),
        operands,
        [kept, kept, depth((texts,)), depth((images,))]
        + [pltpu.SemaphoreType.DMA((2 * rows // COPY_ROWS,))],
    )


def solution(mesh):
    spec = P(("rep", "blk"), None)
    return jax.shard_map(
        local, mesh=mesh, in_specs=(spec, spec), out_specs=(spec, spec), check_vma=False
    )
```

```python
import functools
import math

import jax
import jax.numpy as jnp
from jax import lax
from jax.experimental import pallas as pl
from jax.experimental.pallas import tpu as pltpu
from jax.sharding import PartitionSpec as P

AXIS = "blk"
FIRST_IMAGES = 8
FIRST_TEXTS = 8
LAST_TILE = 256
COPY_ROWS = 128
VMEM_MIB = 32
VMEM = pl.BlockSpec(memory_space=pltpu.VMEM)
ANY = pl.BlockSpec(memory_space=pl.ANY)
LOG2_E = math.log2(math.e)


def send(block, target):
    count = lax.axis_size(AXIS)
    return lax.ppermute(block, AXIS, [(i, target(i) % count) for i in range(count)])


def swap(block, parts):
    return [send(part, lambda i: i ^ 1) for part in jnp.split(block, parts)]


def core():
    return lax.rem(lax.axis_index(AXIS), 2)


def logits(own, others):
    return lax.dot_general(
        own[...], others[...], (((1,), (1,)), ((), ())), preferred_element_type=jnp.float32
    )


def decay(factor, inner_prod):
    return jnp.exp2(LOG2_E - (factor * LOG2_E) * inner_prod)


def product(weight, others):
    return jnp.dot(weight.astype(jnp.bfloat16), others[...], preferred_element_type=jnp.float32)


def add_all(factor, units):
    following = logits(*units[0][:2])
    for k, (_, others, use) in enumerate(units):
        inner_prod = following
        if k + 1 < len(units):
            following = logits(*units[k + 1][:2])
        weight = pl.reciprocal(1.0 + decay(factor, inner_prod), approx=True)
        use(product(weight, others))


def join(visitors, joined):
    if len(visitors) == 1:
        return visitors[0]
    start = 0
    for visitor in visitors:
        joined[pl.ds(start, visitor.shape[0])] = visitor[...]
        start += visitor.shape[0]
    return joined.at[pl.ds(0, start)]


def pick_kernel(image_ref, text_ref, image_head, text_head, far_own, near_own, sems):
    def move(k, source, out):
        return pltpu.make_async_copy(source.at[pl.ds(0, out.shape[0])], out, sems.at[k])

    heads = [move(0, image_ref, image_head), move(1, text_ref, text_head)]
    for head in heads:
        head.start()
    for is_core, (far, near) in enumerate(((image_ref, text_ref), (text_ref, image_ref))):

        @pl.when(core() == is_core)
        def _():
            blocks = [move(2, far, far_own), move(3, near, near_own)]
            for block in blocks:
                block.start()
            for block in blocks:
                block.wait()

    for head in heads:
        head.wait()


def own_kernel(factor, image_ref, text_ref, image_sum, text_sum):
    rows = image_ref.shape[0]
    shape = (rows, rows)
    matched = lax.broadcasted_iota(jnp.int32, shape, 0) == lax.broadcasted_iota(
        jnp.int32, shape, 1
    )
    for own, others, total in ((image_ref, text_ref, image_sum), (text_ref, image_ref, text_sum)):
        chance = 1.0 / (1.0 + decay(factor, logits(own, others)))
        total[...] = product(chance - matched.astype(jnp.float32), others)


def step_kernel(factor, units, sides, *refs):
    is_1 = core().astype(jnp.float32)
    parts = []
    for _, count in units:
        parts.append((refs[0], refs[1 : 1 + count]))
        refs = refs[1 + count :]
    totals = dict(zip(sides, refs))
    sums = dict(zip(sides, refs[len(sides) :]))
    joined = refs[2 * len(sides) :]
    touched = set()

    def add(side, value):
        sums[side][...] = (sums if side in touched else totals)[side][...] + value
        touched.add(side)

    def use(side, value):
        if side < 2:
            add(side, value)
        else:
            add(side - 2, value * (1.0 - is_1))
            add(3 - side, value * is_1)

    add_all(
        factor,
        [
            (own, join(visitors, scratch), functools.partial(use, side))
            for (side, _), (own, visitors), scratch in zip(units, parts, joined)
        ],
    )


def last_kernel(factor, counts, *refs):
    parts = []
    for count in counts:
        parts.append((refs[0], refs[1 : 1 + count], refs[1 + count]))
        refs = refs[2 + count :]
    outs, helds, joined, sems = refs[:2], refs[2:4], refs[4:6], refs[6]
    copies = []

    def use(total, held, out, start, value):
        rows = pl.ds(start, LAST_TILE)
        held[rows] = (total[rows] + value) * factor
        for first in range(start, start + LAST_TILE, COPY_ROWS):
            span = pl.ds(first, COPY_ROWS)
            copies.append(pltpu.make_async_copy(held.at[span], out.at[span], sems.at[len(copies)]))
            copies[-1].start()

    units = []
    for (own, visitors, total), held, out, scratch in zip(parts, helds, outs, joined):
        others = join(visitors, scratch)
        for start in range(0, own.shape[0], LAST_TILE):
            act = functools.partial(use, total, held, out, start)
            units.append((own.at[pl.ds(start, LAST_TILE)], others, act))
    add_all(factor, units)
    for copy in copies:
        copy.wait()


def local(image_embed, text_embed):
    rows, width = image_embed.shape
    dtype = image_embed.dtype
    factor = 2.0 / math.sqrt(width)
    kept = pltpu.VMEM((rows, width), jnp.float32)
    block = pltpu.VMEM((rows, width), dtype)
    grad = jax.ShapeDtypeStruct((rows, width), jnp.float32)

    def call(kernel, outs, operands, scratch=(), aliases=None, in_spec=VMEM):
        return pl.pallas_call(
            kernel,
            out_shape=tuple(outs),
            in_specs=[in_spec] * len(operands),
            out_specs=(ANY if outs[0] is grad else VMEM,) * len(outs),
            scratch_shapes=list(scratch),
            input_output_aliases=aliases or {},
            cost_estimate=pl.CostEstimate(flops=1, bytes_accessed=1, transcendentals=0),
            compiler_params=pltpu.CompilerParams(vmem_limit_bytes=VMEM_MIB << 20),
        )(*operands)

    def depth(visitors):
        return pltpu.VMEM((sum(visitor.shape[0] for visitor in visitors), width), dtype)

    def step(units, sums):
        sides = tuple(sums)
        operands = [ref for _, own, visitors in units for ref in (own, *visitors)]
        counts = [(side, len(visitors)) for side, _, visitors in units]
        return dict(
            zip(
                sides,
                call(
                    functools.partial(step_kernel, factor, counts, sides),
                    [kept] * len(sides),
                    (*operands, *sums.values()),
                    [depth(visitors) for _, _, visitors in units],
                    {len(operands) + k: k for k in range(len(sides))},
                ),
            )
        )

    def after(value, *earlier):
        return lax.optimization_barrier((value, *earlier))[0]

    def next_images(piece):
        return send(piece, lambda i: i - 2)

    def next_texts(piece):
        return send(piece, lambda i: i + 2)

    in_hbm = [pltpu.with_memory_space_constraint(x, pltpu.HBM) for x in (image_embed, text_embed)]
    cut_images, cut_texts = rows * FIRST_IMAGES // 16, rows * FIRST_TEXTS // 16
    heads = (cut_images, cut_texts)
    image_head, text_head, far_own, near_own = call(
        pick_kernel,
        [pltpu.VMEM((head, width), dtype) for head in heads] + [block, block],
        in_hbm,
        [pltpu.SemaphoreType.DMA((4,))],
        in_spec=ANY,
    )
    images, texts = next_images(image_head), next_texts(text_head)
    far = send(far_own, lambda i: i + 3 if i % 2 else i - 3)
    near = swap(near_own, 1)
    later_images = next_images(image_embed[cut_images:])
    later_texts = next_texts(text_embed[cut_texts:])
    sums = call(functools.partial(own_kernel, factor), (kept, kept), (image_embed, text_embed))
    sums = dict(enumerate(sums))
    sums = step([(3, near_own, near)], sums)

    images, texts = after(images, *sums.values()), after(texts, *sums.values())
    swapped_images, swapped_texts = swap(images, 2), swap(texts, 2)
    sums = step(
        [
            (0, image_embed, (texts, *swapped_texts)),
            (1, text_embed, (images, *swapped_images)),
        ],
        sums,
    )
    sums = step([(2, far_own, (after(far, sums[0]),))], sums)

    images, texts = after(later_images, sums[0]), after(later_texts, sums[0])
    swapped_images, swapped_texts = swap(images, 1), swap(texts, 1)
    sums = step(
        [
            (0, image_embed, (texts,)),
            (1, text_embed, (images,)),
        ],
        sums,
    )
    operands = (image_embed, *swapped_texts, sums[0], text_embed, *swapped_images, sums[1])
    return call(
        functools.partial(last_kernel, factor, (1, 1)),
        (grad, grad),
        operands,
        [kept, kept, depth((texts,)), depth((images,))]
        + [pltpu.SemaphoreType.DMA((2 * rows // COPY_ROWS,))],
    )


def solution(mesh):
    spec = P(("rep", "blk"), None)
    return jax.shard_map(
        local, mesh=mesh, in_specs=(spec, spec), out_specs=(spec, spec), check_vma=False
    )
```

```python
import functools
import math

import jax
import jax.numpy as jnp
from jax import lax
from jax.experimental import pallas as pl
from jax.experimental.pallas import tpu as pltpu
from jax.sharding import PartitionSpec as P

AXIS = "blk"
FIRST_IMAGES = 8
FIRST_TEXTS = 8
LAST_TILE = 256
COPY_ROWS = 128
VMEM_MIB = 32
VMEM = pl.BlockSpec(memory_space=pltpu.VMEM)
ANY = pl.BlockSpec(memory_space=pl.ANY)
LOG2_E = math.log2(math.e)


def send(block, target):
    count = lax.axis_size(AXIS)
    return lax.ppermute(block, AXIS, [(i, target(i) % count) for i in range(count)])


def swap(block, parts):
    return [send(part, lambda i: i ^ 1) for part in jnp.split(block, parts)]


def core():
    return lax.rem(lax.axis_index(AXIS), 2)


def logits(own, others):
    return lax.dot_general(
        own[...], others[...], (((1,), (1,)), ((), ())), preferred_element_type=jnp.float32
    )


def decay(factor, inner_prod):
    return jnp.exp2(LOG2_E - (factor * LOG2_E) * inner_prod)


def product(weight, others):
    return jnp.dot(weight.astype(jnp.bfloat16), others[...], preferred_element_type=jnp.float32)


def add_all(factor, units):
    following = logits(*units[0][:2])
    for k, (_, others, use) in enumerate(units):
        inner_prod = following
        if k + 1 < len(units):
            following = logits(*units[k + 1][:2])
        weight = pl.reciprocal(1.0 + decay(factor, inner_prod), approx=True)
        use(product(weight, others))


def join(visitors, joined):
    if len(visitors) == 1:
        return visitors[0]
    start = 0
    for visitor in visitors:
        joined[pl.ds(start, visitor.shape[0])] = visitor[...]
        start += visitor.shape[0]
    return joined.at[pl.ds(0, start)]


def pick_kernel(image_ref, text_ref, *refs):
    outs, sems = refs[:2], refs[2]
    copies = []
    for k, (source, out) in enumerate(zip((image_ref, text_ref), outs)):
        rows = pl.ds(0, out.shape[0])
        copies.append(pltpu.make_async_copy(source.at[rows], out, sems.at[k]))
        copies[-1].start()
    for copy in copies:
        copy.wait()


def core_pick_kernel(image_ref, text_ref, far_own, near_own, sems):
    for is_core, (far, near) in enumerate(((image_ref, text_ref), (text_ref, image_ref))):

        @pl.when(core() == is_core)
        def _():
            copies = [
                pltpu.make_async_copy(far, far_own, sems.at[0]),
                pltpu.make_async_copy(near, near_own, sems.at[1]),
            ]
            for copy in copies:
                copy.start()
            for copy in copies:
                copy.wait()


def own_kernel(factor, image_ref, text_ref, image_sum, text_sum):
    rows = image_ref.shape[0]
    shape = (rows, rows)
    matched = lax.broadcasted_iota(jnp.int32, shape, 0) == lax.broadcasted_iota(
        jnp.int32, shape, 1
    )
    for own, others, total in ((image_ref, text_ref, image_sum), (text_ref, image_ref, text_sum)):
        chance = 1.0 / (1.0 + decay(factor, logits(own, others)))
        total[...] = product(chance - matched.astype(jnp.float32), others)


def step_kernel(factor, units, sides, *refs):
    is_1 = core().astype(jnp.float32)
    parts = []
    for _, count in units:
        parts.append((refs[0], refs[1 : 1 + count]))
        refs = refs[1 + count :]
    totals = dict(zip(sides, refs))
    sums = dict(zip(sides, refs[len(sides) :]))
    joined = refs[2 * len(sides) :]
    touched = set()

    def add(side, value):
        sums[side][...] = (sums if side in touched else totals)[side][...] + value
        touched.add(side)

    def use(side, value):
        if side < 2:
            add(side, value)
        else:
            add(side - 2, value * (1.0 - is_1))
            add(3 - side, value * is_1)

    def meet(side, own, visitors, scratch):
        others = join(visitors, scratch)
        if side == 3:
            others = others.at[pl.ds((1 - core()) * own.shape[0], own.shape[0])]
        return own, others, functools.partial(use, side)

    add_all(
        factor,
        [
            meet(side, own, visitors, scratch)
            for (side, _), (own, visitors), scratch in zip(units, parts, joined)
        ],
    )


def last_kernel(factor, counts, *refs):
    parts = []
    for count in counts:
        parts.append((refs[0], refs[1 : 1 + count], refs[1 + count]))
        refs = refs[2 + count :]
    outs, helds, joined, sems = refs[:2], refs[2:4], refs[4:6], refs[6]
    copies = []

    def use(total, held, out, start, value):
        rows = pl.ds(start, LAST_TILE)
        held[rows] = (total[rows] + value) * factor
        for first in range(start, start + LAST_TILE, COPY_ROWS):
            span = pl.ds(first, COPY_ROWS)
            copies.append(pltpu.make_async_copy(held.at[span], out.at[span], sems.at[len(copies)]))
            copies[-1].start()

    units = []
    for (own, visitors, total), held, out, scratch in zip(parts, helds, outs, joined):
        others = join(visitors, scratch)
        for start in range(0, own.shape[0], LAST_TILE):
            act = functools.partial(use, total, held, out, start)
            units.append((own.at[pl.ds(start, LAST_TILE)], others, act))
    add_all(factor, units)
    for copy in copies:
        copy.wait()


def local(image_embed, text_embed):
    rows, width = image_embed.shape
    dtype = image_embed.dtype
    factor = 2.0 / math.sqrt(width)
    kept = pltpu.VMEM((rows, width), jnp.float32)
    block = pltpu.VMEM((rows, width), dtype)
    grad = jax.ShapeDtypeStruct((rows, width), jnp.float32)

    def call(kernel, outs, operands, scratch=(), aliases=None, in_spec=VMEM):
        return pl.pallas_call(
            kernel,
            out_shape=tuple(outs),
            in_specs=[in_spec] * len(operands),
            out_specs=(ANY if outs[0] is grad else VMEM,) * len(outs),
            scratch_shapes=list(scratch),
            input_output_aliases=aliases or {},
            cost_estimate=pl.CostEstimate(flops=1, bytes_accessed=1, transcendentals=0),
            compiler_params=pltpu.CompilerParams(vmem_limit_bytes=VMEM_MIB << 20),
        )(*operands)

    def depth(visitors):
        return pltpu.VMEM((sum(visitor.shape[0] for visitor in visitors), width), dtype)

    def step(units, sums):
        sides = tuple(sums)
        operands = [ref for _, own, visitors in units for ref in (own, *visitors)]
        counts = [(side, len(visitors)) for side, _, visitors in units]
        return dict(
            zip(
                sides,
                call(
                    functools.partial(step_kernel, factor, counts, sides),
                    [kept] * len(sides),
                    (*operands, *sums.values()),
                    [depth(visitors) for _, _, visitors in units],
                    {len(operands) + k: k for k in range(len(sides))},
                ),
            )
        )

    def after(value, *earlier):
        return lax.optimization_barrier((value, *earlier))[0]

    def next_images(piece):
        return send(piece, lambda i: i - 2)

    def next_texts(piece):
        return send(piece, lambda i: i + 2)

    in_hbm = [pltpu.with_memory_space_constraint(x, pltpu.HBM) for x in (image_embed, text_embed)]
    cut_images, cut_texts = rows * FIRST_IMAGES // 16, rows * FIRST_TEXTS // 16
    heads = (cut_images, cut_texts)
    image_head, text_head = call(
        pick_kernel,
        [pltpu.VMEM((head, width), dtype) for head in heads],
        in_hbm,
        [pltpu.SemaphoreType.DMA((2,))],
        in_spec=ANY,
    )
    images, texts = next_images(image_head), next_texts(text_head)
    far_own, near_own = call(
        core_pick_kernel, [block, block], in_hbm, [pltpu.SemaphoreType.DMA((2,))], in_spec=ANY
    )
    far = send(far_own, lambda i: i + 3 if i % 2 else i - 3)
    pairs = [[i, i + 1] for i in range(0, lax.axis_size(AXIS), 2)]
    near = [lax.all_gather(near_own, AXIS, axis_index_groups=pairs, tiled=True)]
    later_images = next_images(image_embed[cut_images:])
    later_texts = next_texts(text_embed[cut_texts:])
    sums = call(functools.partial(own_kernel, factor), (kept, kept), (image_embed, text_embed))
    sums = dict(enumerate(sums))

    images, texts = after(images, *sums.values()), after(texts, *sums.values())
    swapped_images, swapped_texts = swap(images, 2), swap(texts, 2)
    sums = step(
        [
            (3, near_own, near),
            (0, image_embed, (texts, *swapped_texts)),
            (1, text_embed, (images, *swapped_images)),
        ],
        sums,
    )
    sums = step([(2, far_own, (after(far, sums[0]),))], sums)

    images, texts = after(later_images, sums[0]), after(later_texts, sums[0])
    swapped_images, swapped_texts = swap(images, 1), swap(texts, 1)
    sums = step(
        [
            (0, image_embed, (texts,)),
            (1, text_embed, (images,)),
        ],
        sums,
    )
    operands = (image_embed, *swapped_texts, sums[0], text_embed, *swapped_images, sums[1])
    return call(
        functools.partial(last_kernel, factor, (1, 1)),
        (grad, grad),
        operands,
        [kept, kept, depth((texts,)), depth((images,))]
        + [pltpu.SemaphoreType.DMA((2 * rows // COPY_ROWS,))],
    )


def solution(mesh):
    spec = P(("rep", "blk"), None)
    return jax.shard_map(
        local, mesh=mesh, in_specs=(spec, spec), out_specs=(spec, spec), check_vma=False
    )
```

```python
import functools
import math

import jax
import jax.numpy as jnp
from jax import lax
from jax.experimental import pallas as pl
from jax.experimental.pallas import tpu as pltpu
from jax.sharding import PartitionSpec as P

AXIS = "blk"
FIRST_IMAGES = 8
FIRST_TEXTS = 8
NEAR_PARTS = 1
LAST_TILE = 256
COPY_ROWS = 128
VMEM_MIB = 32
VMEM = pl.BlockSpec(memory_space=pltpu.VMEM)
ANY = pl.BlockSpec(memory_space=pl.ANY)
LOG2_E = math.log2(math.e)


def send(block, target):
    count = lax.axis_size(AXIS)
    return lax.ppermute(block, AXIS, [(i, target(i) % count) for i in range(count)])


def swap(block, parts):
    return [send(part, lambda i: i ^ 1) for part in jnp.split(block, parts)]


def core():
    return lax.rem(lax.axis_index(AXIS), 2)


def logits(own, others):
    return lax.dot_general(
        own[...], others[...], (((1,), (1,)), ((), ())), preferred_element_type=jnp.float32
    )


def decay(factor, inner_prod):
    return jnp.exp2(LOG2_E - (factor * LOG2_E) * inner_prod)


def product(weight, others):
    return jnp.dot(weight.astype(jnp.bfloat16), others[...], preferred_element_type=jnp.float32)


def add_all(factor, units):
    following = logits(*units[0][:2])
    for k, (_, others, use) in enumerate(units):
        inner_prod = following
        if k + 1 < len(units):
            following = logits(*units[k + 1][:2])
        weight = pl.reciprocal(1.0 + decay(factor, inner_prod), approx=True)
        use(product(weight, others))


def join(visitors, joined):
    if len(visitors) == 1:
        return visitors[0]
    start = 0
    for visitor in visitors:
        joined[pl.ds(start, visitor.shape[0])] = visitor[...]
        start += visitor.shape[0]
    return joined.at[pl.ds(0, start)]


def pick_kernel(image_ref, text_ref, image_head, text_head, far_own, near_own, sems):
    def move(k, source, out):
        return pltpu.make_async_copy(source.at[pl.ds(0, out.shape[0])], out, sems.at[k])

    heads = [move(0, image_ref, image_head), move(1, text_ref, text_head)]
    for head in heads:
        head.start()
    for is_core, (far, near) in enumerate(((image_ref, text_ref), (text_ref, image_ref))):

        @pl.when(core() == is_core)
        def _():
            blocks = [move(2, far, far_own), move(3, near, near_own)]
            for block in blocks:
                block.start()
            for block in blocks:
                block.wait()

    for head in heads:
        head.wait()


def own_kernel(factor, image_ref, text_ref, near_own, *refs):
    near, (image_sum, text_sum, joined) = refs[:NEAR_PARTS], refs[NEAR_PARTS:]
    rows = image_ref.shape[0]
    shape = (rows, rows)
    matched = lax.broadcasted_iota(jnp.int32, shape, 0) == lax.broadcasted_iota(
        jnp.int32, shape, 1
    )
    for own, others, total in ((image_ref, text_ref, image_sum), (text_ref, image_ref, text_sum)):
        chance = 1.0 / (1.0 + decay(factor, logits(own, others)))
        total[...] = product(chance - matched.astype(jnp.float32), others)
    is_1 = core().astype(jnp.float32)

    def use(value):
        image_sum[...] += value * is_1
        text_sum[...] += value * (1.0 - is_1)

    add_all(factor, [(near_own, join(near, joined), use)])


def step_kernel(factor, units, sides, *refs):
    is_1 = core().astype(jnp.float32)
    parts = []
    for _, count in units:
        parts.append((refs[0], refs[1 : 1 + count]))
        refs = refs[1 + count :]
    totals = dict(zip(sides, refs))
    sums = dict(zip(sides, refs[len(sides) :]))
    joined = refs[2 * len(sides) :]
    touched = set()

    def add(side, value):
        sums[side][...] = (sums if side in touched else totals)[side][...] + value
        touched.add(side)

    def use(side, value):
        if side < 2:
            add(side, value)
        else:
            add(side - 2, value * (1.0 - is_1))
            add(3 - side, value * is_1)

    add_all(
        factor,
        [
            (own, join(visitors, scratch), functools.partial(use, side))
            for (side, _), (own, visitors), scratch in zip(units, parts, joined)
        ],
    )


def last_kernel(factor, counts, *refs):
    parts = []
    for count in counts:
        parts.append((refs[0], refs[1 : 1 + count], refs[1 + count]))
        refs = refs[2 + count :]
    outs, helds, joined, sems = refs[:2], refs[2:4], refs[4:6], refs[6]
    copies = []

    def use(total, held, out, start, value):
        rows = pl.ds(start, LAST_TILE)
        held[rows] = (total[rows] + value) * factor
        for first in range(start, start + LAST_TILE, COPY_ROWS):
            span = pl.ds(first, COPY_ROWS)
            copies.append(pltpu.make_async_copy(held.at[span], out.at[span], sems.at[len(copies)]))
            copies[-1].start()

    units = []
    for (own, visitors, total), held, out, scratch in zip(parts, helds, outs, joined):
        others = join(visitors, scratch)
        for start in range(0, own.shape[0], LAST_TILE):
            act = functools.partial(use, total, held, out, start)
            units.append((own.at[pl.ds(start, LAST_TILE)], others, act))
    add_all(factor, units)
    for copy in copies:
        copy.wait()


def local(image_embed, text_embed):
    rows, width = image_embed.shape
    dtype = image_embed.dtype
    factor = 2.0 / math.sqrt(width)
    kept = pltpu.VMEM((rows, width), jnp.float32)
    block = pltpu.VMEM((rows, width), dtype)
    grad = jax.ShapeDtypeStruct((rows, width), jnp.float32)

    def call(kernel, outs, operands, scratch=(), aliases=None, in_spec=VMEM):
        return pl.pallas_call(
            kernel,
            out_shape=tuple(outs),
            in_specs=[in_spec] * len(operands),
            out_specs=(ANY if outs[0] is grad else VMEM,) * len(outs),
            scratch_shapes=list(scratch),
            input_output_aliases=aliases or {},
            cost_estimate=pl.CostEstimate(flops=1, bytes_accessed=1, transcendentals=0),
            compiler_params=pltpu.CompilerParams(vmem_limit_bytes=VMEM_MIB << 20),
        )(*operands)

    def depth(visitors):
        return pltpu.VMEM((sum(visitor.shape[0] for visitor in visitors), width), dtype)

    def step(units, sums):
        sides = tuple(sums)
        operands = [ref for _, own, visitors in units for ref in (own, *visitors)]
        counts = [(side, len(visitors)) for side, _, visitors in units]
        return dict(
            zip(
                sides,
                call(
                    functools.partial(step_kernel, factor, counts, sides),
                    [kept] * len(sides),
                    (*operands, *sums.values()),
                    [depth(visitors) for _, _, visitors in units],
                    {len(operands) + k: k for k in range(len(sides))},
                ),
            )
        )

    def after(value, *earlier):
        return lax.optimization_barrier((value, *earlier))[0]

    def next_images(piece):
        return send(piece, lambda i: i - 2)

    def next_texts(piece):
        return send(piece, lambda i: i + 2)

    in_hbm = [pltpu.with_memory_space_constraint(x, pltpu.HBM) for x in (image_embed, text_embed)]
    cut_images, cut_texts = rows * FIRST_IMAGES // 16, rows * FIRST_TEXTS // 16
    heads = (cut_images, cut_texts)
    image_head, text_head, far_own, near_own = call(
        pick_kernel,
        [pltpu.VMEM((head, width), dtype) for head in heads] + [block, block],
        in_hbm,
        [pltpu.SemaphoreType.DMA((4,))],
        in_spec=ANY,
    )
    images, texts = next_images(image_head), next_texts(text_head)
    far = send(far_own, lambda i: i + 3 if i % 2 else i - 3)
    near = swap(near_own, 1)
    later_images = next_images(image_embed[cut_images:])
    later_texts = next_texts(text_embed[cut_texts:])
    sums = call(
        functools.partial(own_kernel, factor),
        (kept, kept),
        (image_embed, text_embed, near_own, *near),
        [block],
    )
    sums = dict(enumerate(sums))

    images, texts = after(images, *sums.values()), after(texts, *sums.values())
    swapped_images, swapped_texts = swap(images, 2), swap(texts, 2)
    sums = step(
        [
            (0, image_embed, (texts, *swapped_texts)),
            (1, text_embed, (images, *swapped_images)),
        ],
        sums,
    )
    sums = step([(2, far_own, (after(far, sums[0]),))], sums)

    images, texts = after(later_images, sums[0]), after(later_texts, sums[0])
    swapped_images, swapped_texts = swap(images, 1), swap(texts, 1)
    sums = step(
        [
            (0, image_embed, (texts,)),
            (1, text_embed, (images,)),
        ],
        sums,
    )
    operands = (image_embed, *swapped_texts, sums[0], text_embed, *swapped_images, sums[1])
    return call(
        functools.partial(last_kernel, factor, (1, 1)),
        (grad, grad),
        operands,
        [kept, kept, depth((texts,)), depth((images,))]
        + [pltpu.SemaphoreType.DMA((2 * rows // COPY_ROWS,))],
    )


def solution(mesh):
    spec = P(("rep", "blk"), None)
    return jax.shard_map(
        local, mesh=mesh, in_specs=(spec, spec), out_specs=(spec, spec), check_vma=False
    )
```

```python
import functools
import math

import jax
import jax.numpy as jnp
from jax import lax
from jax.experimental import pallas as pl
from jax.experimental.pallas import tpu as pltpu
from jax.sharding import PartitionSpec as P

AXIS = "blk"
FIRST_IMAGES = 8
FIRST_TEXTS = 8
NEAR_PARTS = 1
LAST_TILE = 256
COPY_ROWS = 128
VMEM_MIB = 32
VMEM = pl.BlockSpec(memory_space=pltpu.VMEM)
ANY = pl.BlockSpec(memory_space=pl.ANY)
LOG2_E = math.log2(math.e)


def send(block, target):
    count = lax.axis_size(AXIS)
    return lax.ppermute(block, AXIS, [(i, target(i) % count) for i in range(count)])


def swap(block, parts):
    return [send(part, lambda i: i ^ 1) for part in jnp.split(block, parts)]


def core():
    return lax.rem(lax.axis_index(AXIS), 2)


def logits(own, others):
    return lax.dot_general(
        own[...], others[...], (((1,), (1,)), ((), ())), preferred_element_type=jnp.float32
    )


def decay(factor, inner_prod):
    return jnp.exp2(LOG2_E - (factor * LOG2_E) * inner_prod)


def product(weight, others):
    return jnp.dot(weight.astype(jnp.bfloat16), others[...], preferred_element_type=jnp.float32)


def add_all(factor, units):
    following = logits(*units[0][:2])
    for k, (_, others, use) in enumerate(units):
        inner_prod = following
        if k + 1 < len(units):
            following = logits(*units[k + 1][:2])
        weight = pl.reciprocal(1.0 + decay(factor, inner_prod), approx=True)
        use(product(weight, others))


def join(visitors, joined):
    if len(visitors) == 1:
        return visitors[0]
    start = 0
    for visitor in visitors:
        joined[pl.ds(start, visitor.shape[0])] = visitor[...]
        start += visitor.shape[0]
    return joined.at[pl.ds(0, start)]


def pick_kernel(image_ref, text_ref, image_head, text_head, near_own, sems):
    def move(k, source, out):
        return pltpu.make_async_copy(source.at[pl.ds(0, out.shape[0])], out, sems.at[k])

    heads = [move(0, image_ref, image_head), move(1, text_ref, text_head)]
    for head in heads:
        head.start()
    for is_core, near in enumerate((text_ref, image_ref)):

        @pl.when(core() == is_core)
        def _():
            block = move(2, near, near_own)
            block.start()
            block.wait()

    for head in heads:
        head.wait()


def far_pick_kernel(image_ref, text_ref, *refs):
    far_own, sem = refs[-2:]
    for is_core, far in enumerate((image_ref, text_ref)):

        @pl.when(core() == is_core)
        def _():
            copy = pltpu.make_async_copy(far, far_own, sem)
            copy.start()
            copy.wait()


def own_kernel(factor, image_ref, text_ref, near_own, *refs):
    near, (image_sum, text_sum, joined) = refs[:NEAR_PARTS], refs[NEAR_PARTS:]
    rows = image_ref.shape[0]
    shape = (rows, rows)
    matched = lax.broadcasted_iota(jnp.int32, shape, 0) == lax.broadcasted_iota(
        jnp.int32, shape, 1
    )
    for own, others, total in ((image_ref, text_ref, image_sum), (text_ref, image_ref, text_sum)):
        chance = 1.0 / (1.0 + decay(factor, logits(own, others)))
        total[...] = product(chance - matched.astype(jnp.float32), others)
    is_1 = core().astype(jnp.float32)

    def use(value):
        image_sum[...] += value * is_1
        text_sum[...] += value * (1.0 - is_1)

    add_all(factor, [(near_own, join(near, joined), use)])


def step_kernel(factor, units, sides, *refs):
    is_1 = core().astype(jnp.float32)
    parts = []
    for _, count in units:
        parts.append((refs[0], refs[1 : 1 + count]))
        refs = refs[1 + count :]
    totals = dict(zip(sides, refs))
    sums = dict(zip(sides, refs[len(sides) :]))
    joined = refs[2 * len(sides) :]
    touched = set()

    def add(side, value):
        sums[side][...] = (sums if side in touched else totals)[side][...] + value
        touched.add(side)

    def use(side, value):
        if side < 2:
            add(side, value)
        else:
            add(side - 2, value * (1.0 - is_1))
            add(3 - side, value * is_1)

    add_all(
        factor,
        [
            (own, join(visitors, scratch), functools.partial(use, side))
            for (side, _), (own, visitors), scratch in zip(units, parts, joined)
        ],
    )


def last_kernel(factor, counts, far_own, far, *refs):
    parts = []
    for count in counts:
        parts.append((refs[0], refs[1 : 1 + count], refs[1 + count]))
        refs = refs[2 + count :]
    outs, helds, joined, sems = refs[:2], refs[2:4], refs[4:6], refs[6]
    starts = range(0, far_own.shape[0], LAST_TILE)
    is_1 = core().astype(jnp.float32)
    copies = []

    def use_far(start, value):
        rows = pl.ds(start, LAST_TILE)
        helds[0][rows] = parts[0][2][rows] + value * (1.0 - is_1)
        helds[1][rows] = parts[1][2][rows] + value * is_1

    def use(held, out, start, value):
        rows = pl.ds(start, LAST_TILE)
        held[rows] = (held[rows] + value) * factor
        for first in range(start, start + LAST_TILE, COPY_ROWS):
            span = pl.ds(first, COPY_ROWS)
            copies.append(pltpu.make_async_copy(held.at[span], out.at[span], sems.at[len(copies)]))
            copies[-1].start()

    def unit(own, others, start, act, *args):
        return (own.at[pl.ds(start, LAST_TILE)], others, functools.partial(act, *args, start))

    units = [unit(far_own, far, start, use_far) for start in starts]
    for (own, visitors, _), held, out, scratch in zip(parts, helds, outs, joined):
        others = join(visitors, scratch)
        units += [unit(own, others, start, use, held, out) for start in starts]
    add_all(factor, units)
    for copy in copies:
        copy.wait()


def local(image_embed, text_embed):
    rows, width = image_embed.shape
    dtype = image_embed.dtype
    factor = 2.0 / math.sqrt(width)
    kept = pltpu.VMEM((rows, width), jnp.float32)
    block = pltpu.VMEM((rows, width), dtype)
    grad = jax.ShapeDtypeStruct((rows, width), jnp.float32)

    def call(kernel, outs, operands, scratch=(), aliases=None, in_spec=VMEM):
        return pl.pallas_call(
            kernel,
            out_shape=tuple(outs),
            in_specs=[in_spec] * len(operands),
            out_specs=(ANY if outs[0] is grad else VMEM,) * len(outs),
            scratch_shapes=list(scratch),
            input_output_aliases=aliases or {},
            cost_estimate=pl.CostEstimate(flops=1, bytes_accessed=1, transcendentals=0),
            compiler_params=pltpu.CompilerParams(vmem_limit_bytes=VMEM_MIB << 20),
        )(*operands)

    def depth(visitors):
        return pltpu.VMEM((sum(visitor.shape[0] for visitor in visitors), width), dtype)

    def step(units, sums):
        sides = tuple(sums)
        operands = [ref for _, own, visitors in units for ref in (own, *visitors)]
        counts = [(side, len(visitors)) for side, _, visitors in units]
        return dict(
            zip(
                sides,
                call(
                    functools.partial(step_kernel, factor, counts, sides),
                    [kept] * len(sides),
                    (*operands, *sums.values()),
                    [depth(visitors) for _, _, visitors in units],
                    {len(operands) + k: k for k in range(len(sides))},
                ),
            )
        )

    def after(value, *earlier):
        return lax.optimization_barrier((value, *earlier))[0]

    def next_images(piece):
        return send(piece, lambda i: i - 2)

    def next_texts(piece):
        return send(piece, lambda i: i + 2)

    in_hbm = [pltpu.with_memory_space_constraint(x, pltpu.HBM) for x in (image_embed, text_embed)]
    cut_images, cut_texts = rows * FIRST_IMAGES // 16, rows * FIRST_TEXTS // 16
    heads = (cut_images, cut_texts)
    image_head, text_head, near_own = call(
        pick_kernel,
        [pltpu.VMEM((head, width), dtype) for head in heads] + [block],
        in_hbm,
        [pltpu.SemaphoreType.DMA((3,))],
        in_spec=ANY,
    )
    images, texts = next_images(image_head), next_texts(text_head)
    near = swap(near_own, 1)
    (far_own,) = call(
        far_pick_kernel, [block], in_hbm, [pltpu.SemaphoreType.DMA], in_spec=ANY
    )
    far = send(far_own, lambda i: i + 3 if i % 2 else i - 3)
    later_images = next_images(image_embed[cut_images:])
    later_texts = next_texts(text_embed[cut_texts:])
    sums = call(
        functools.partial(own_kernel, factor),
        (kept, kept),
        (image_embed, text_embed, near_own, *near),
        [block],
    )
    sums = dict(enumerate(sums))

    images, texts = after(images, *sums.values()), after(texts, *sums.values())
    swapped_images, swapped_texts = swap(images, 2), swap(texts, 2)
    sums = step(
        [
            (0, image_embed, (texts, *swapped_texts)),
            (1, text_embed, (images, *swapped_images)),
        ],
        sums,
    )

    images, texts = after(later_images, sums[0]), after(later_texts, sums[0])
    swapped_images, swapped_texts = swap(images, 1), swap(texts, 1)
    sums = step(
        [
            (0, image_embed, (texts,)),
            (1, text_embed, (images,)),
        ],
        sums,
    )
    operands = (image_embed, *swapped_texts, sums[0], text_embed, *swapped_images, sums[1])
    operands = (far_own, far, *operands)
    return call(
        functools.partial(last_kernel, factor, (1, 1)),
        (grad, grad),
        operands,
        [kept, kept, depth((texts,)), depth((images,))]
        + [pltpu.SemaphoreType.DMA((2 * rows // COPY_ROWS,))],
    )


def solution(mesh):
    spec = P(("rep", "blk"), None)
    return jax.shard_map(
        local, mesh=mesh, in_specs=(spec, spec), out_specs=(spec, spec), check_vma=False
    )
```

```python
import functools
import math

import jax
import jax.numpy as jnp
from jax import lax
from jax.experimental import pallas as pl
from jax.experimental.pallas import tpu as pltpu
from jax.sharding import PartitionSpec as P

AXIS = "blk"
FIRST_IMAGES = 8
FIRST_TEXTS = 8
NEAR_PARTS = 1
LAST_TILE = 256
COPY_ROWS = 128
VMEM_MIB = 32
VMEM = pl.BlockSpec(memory_space=pltpu.VMEM)
ANY = pl.BlockSpec(memory_space=pl.ANY)
LOG2_E = math.log2(math.e)


def send(block, target):
    count = lax.axis_size(AXIS)
    return lax.ppermute(block, AXIS, [(i, target(i) % count) for i in range(count)])


def swap(block, parts):
    return [send(part, lambda i: i ^ 1) for part in jnp.split(block, parts)]


def core():
    return lax.rem(lax.axis_index(AXIS), 2)


def logits(own, others):
    return lax.dot_general(
        own[...], others[...], (((1,), (1,)), ((), ())), preferred_element_type=jnp.float32
    )


def decay(factor, inner_prod):
    return jnp.exp2(LOG2_E - (factor * LOG2_E) * inner_prod)


def product(weight, others):
    return jnp.dot(weight.astype(jnp.bfloat16), others[...], preferred_element_type=jnp.float32)


def add_all(factor, units):
    following = logits(*units[0][:2])
    for k, (_, others, use) in enumerate(units):
        inner_prod = following
        if k + 1 < len(units):
            following = logits(*units[k + 1][:2])
        weight = pl.reciprocal(1.0 + decay(factor, inner_prod), approx=True)
        use(product(weight, others))


def join(visitors, joined):
    if len(visitors) == 1:
        return visitors[0]
    start = 0
    for visitor in visitors:
        joined[pl.ds(start, visitor.shape[0])] = visitor[...]
        start += visitor.shape[0]
    return joined.at[pl.ds(0, start)]


def pick_kernel(image_ref, text_ref, image_head, text_head, far_own, near_own, sems):
    def move(k, source, out):
        return pltpu.make_async_copy(source.at[pl.ds(0, out.shape[0])], out, sems.at[k])

    heads = [move(0, image_ref, image_head), move(1, text_ref, text_head)]
    for head in heads:
        head.start()
    for is_core, (far, near) in enumerate(((image_ref, text_ref), (text_ref, image_ref))):

        @pl.when(core() == is_core)
        def _():
            blocks = [move(2, far, far_own), move(3, near, near_own)]
            for block in blocks:
                block.start()
            for block in blocks:
                block.wait()

    for head in heads:
        head.wait()


def own_kernel(factor, image_ref, text_ref, near_own, *refs):
    near, (image_sum, text_sum, joined) = refs[:NEAR_PARTS], refs[NEAR_PARTS:]
    rows = image_ref.shape[0]
    shape = (rows, rows)
    matched = lax.broadcasted_iota(jnp.int32, shape, 0) == lax.broadcasted_iota(
        jnp.int32, shape, 1
    )
    for own, others, total in ((image_ref, text_ref, image_sum), (text_ref, image_ref, text_sum)):
        chance = 1.0 / (1.0 + decay(factor, logits(own, others)))
        total[...] = product(chance - matched.astype(jnp.float32), others)
    is_1 = core().astype(jnp.float32)

    def use(value):
        image_sum[...] += value * is_1
        text_sum[...] += value * (1.0 - is_1)

    add_all(factor, [(near_own, join(near, joined), use)])


def step_kernel(factor, scale, units, sides, *refs):
    is_1 = core().astype(jnp.float32)
    parts = []
    for _, count in units:
        parts.append((refs[0], refs[1 : 1 + count]))
        refs = refs[1 + count :]
    totals = dict(zip(sides, refs))
    sums = dict(zip(sides, refs[len(sides) :]))
    joined = refs[2 * len(sides) :]
    touched = set()

    def add(side, value):
        total = (sums if side in touched else totals)[side][...]
        sums[side][...] = (total + value) * scale
        touched.add(side)

    def use(side, value):
        if side < 2:
            add(side, value)
        else:
            add(side - 2, value * (1.0 - is_1))
            add(3 - side, value * is_1)

    add_all(
        factor,
        [
            (own, join(visitors, scratch), functools.partial(use, side))
            for (side, _), (own, visitors), scratch in zip(units, parts, joined)
        ],
    )


def last_kernel(factor, far_own, far, *refs):
    sums, outs, held, sems = refs[:2], refs[2:4], refs[4], refs[5]
    firsts = range(0, far_own.shape[0], COPY_ROWS)

    def whole(side):
        return pltpu.make_async_copy(sums[side], outs[side], sems.at[len(firsts)])

    def part(side, first):
        span = pl.ds(first, COPY_ROWS)
        return pltpu.make_async_copy(held.at[span], outs[side].at[span], sems.at[first // COPY_ROWS])

    def on_each_core(act):
        for is_core in (0, 1):
            pl.when(core() == is_core)(functools.partial(act, is_core))

    def use(start, value):
        def add(side):
            rows = pl.ds(start, LAST_TILE)
            held[rows] = sums[side][rows] + value * factor
            for first in range(start, start + LAST_TILE, COPY_ROWS):
                part(side, first).start()

        on_each_core(add)

    def finish(side):
        whole(1 - side).wait()
        for first in firsts:
            part(side, first).wait()

    on_each_core(lambda side: whole(1 - side).start())
    units = []
    for start in range(0, far_own.shape[0], LAST_TILE):
        units.append((far_own.at[pl.ds(start, LAST_TILE)], far, functools.partial(use, start)))
    add_all(factor, units)
    on_each_core(finish)


def local(image_embed, text_embed):
    rows, width = image_embed.shape
    dtype = image_embed.dtype
    factor = 2.0 / math.sqrt(width)
    kept = pltpu.VMEM((rows, width), jnp.float32)
    block = pltpu.VMEM((rows, width), dtype)
    grad = jax.ShapeDtypeStruct((rows, width), jnp.float32)

    def call(kernel, outs, operands, scratch=(), aliases=None, in_spec=VMEM):
        return pl.pallas_call(
            kernel,
            out_shape=tuple(outs),
            in_specs=[in_spec] * len(operands),
            out_specs=(ANY if outs[0] is grad else VMEM,) * len(outs),
            scratch_shapes=list(scratch),
            input_output_aliases=aliases or {},
            cost_estimate=pl.CostEstimate(flops=1, bytes_accessed=1, transcendentals=0),
            compiler_params=pltpu.CompilerParams(vmem_limit_bytes=VMEM_MIB << 20),
        )(*operands)

    def depth(visitors):
        return pltpu.VMEM((sum(visitor.shape[0] for visitor in visitors), width), dtype)

    def step(units, sums, scale=1.0):
        sides = tuple(sums)
        operands = [ref for _, own, visitors in units for ref in (own, *visitors)]
        counts = [(side, len(visitors)) for side, _, visitors in units]
        return dict(
            zip(
                sides,
                call(
                    functools.partial(step_kernel, factor, scale, counts, sides),
                    [kept] * len(sides),
                    (*operands, *sums.values()),
                    [depth(visitors) for _, _, visitors in units],
                    {len(operands) + k: k for k in range(len(sides))},
                ),
            )
        )

    def after(value, *earlier):
        return lax.optimization_barrier((value, *earlier))[0]

    def next_images(piece):
        return send(piece, lambda i: i - 2)

    def next_texts(piece):
        return send(piece, lambda i: i + 2)

    in_hbm = [pltpu.with_memory_space_constraint(x, pltpu.HBM) for x in (image_embed, text_embed)]
    cut_images, cut_texts = rows * FIRST_IMAGES // 16, rows * FIRST_TEXTS // 16
    heads = (cut_images, cut_texts)
    image_head, text_head, far_own, near_own = call(
        pick_kernel,
        [pltpu.VMEM((head, width), dtype) for head in heads] + [block, block],
        in_hbm,
        [pltpu.SemaphoreType.DMA((4,))],
        in_spec=ANY,
    )
    images, texts = next_images(image_head), next_texts(text_head)
    far = send(far_own, lambda i: i + 3 if i % 2 else i - 3)
    near = swap(near_own, 1)
    later_images = next_images(image_embed[cut_images:])
    later_texts = next_texts(text_embed[cut_texts:])
    sums = call(
        functools.partial(own_kernel, factor),
        (kept, kept),
        (image_embed, text_embed, near_own, *near),
        [block],
    )
    sums = dict(enumerate(sums))

    images, texts = after(images, *sums.values()), after(texts, *sums.values())
    swapped_images, swapped_texts = swap(images, 2), swap(texts, 2)
    sums = step(
        [
            (0, image_embed, (texts, *swapped_texts)),
            (1, text_embed, (images, *swapped_images)),
        ],
        sums,
    )

    images, texts = after(later_images, sums[0]), after(later_texts, sums[0])
    swapped_images, swapped_texts = swap(images, 1), swap(texts, 1)
    sums = step(
        [
            (0, image_embed, (texts,)),
            (1, text_embed, (images,)),
        ],
        sums,
    )
    sums = step(
        [(0, image_embed, swapped_texts), (1, text_embed, swapped_images)], sums, scale=factor
    )
    return call(
        functools.partial(last_kernel, factor),
        (grad, grad),
        (far_own, after(far, sums[0]), sums[0], sums[1]),
        [kept, pltpu.SemaphoreType.DMA((rows // COPY_ROWS + 1,))],
    )


def solution(mesh):
    spec = P(("rep", "blk"), None)
    return jax.shard_map(
        local, mesh=mesh, in_specs=(spec, spec), out_specs=(spec, spec), check_vma=False
    )
```

```python
import functools
import math

import jax
import jax.numpy as jnp
from jax import lax
from jax.experimental import pallas as pl
from jax.experimental.pallas import tpu as pltpu
from jax.sharding import PartitionSpec as P

AXIS = "blk"
FIRST_IMAGES = 8
FIRST_TEXTS = 8
NEAR_PARTS = 1
LAST_TILE = 256
COPY_ROWS = 128
VMEM_MIB = 32
VMEM = pl.BlockSpec(memory_space=pltpu.VMEM)
ANY = pl.BlockSpec(memory_space=pl.ANY)
LOG2_E = math.log2(math.e)


def send(block, target):
    count = lax.axis_size(AXIS)
    return lax.ppermute(block, AXIS, [(i, target(i) % count) for i in range(count)])


def swap(block, parts):
    return [send(part, lambda i: i ^ 1) for part in jnp.split(block, parts)]


def core():
    return lax.rem(lax.axis_index(AXIS), 2)


def logits(own, others):
    return lax.dot_general(
        own[...], others[...], (((1,), (1,)), ((), ())), preferred_element_type=jnp.float32
    )


def decay(factor, inner_prod):
    return jnp.exp2(LOG2_E - (factor * LOG2_E) * inner_prod)


def product(weight, others):
    return jnp.dot(weight.astype(jnp.bfloat16), others[...], preferred_element_type=jnp.float32)


def add_all(factor, units):
    following = logits(*units[0][:2])
    for k, (_, others, use) in enumerate(units):
        inner_prod = following
        if k + 1 < len(units):
            following = logits(*units[k + 1][:2])
        weight = pl.reciprocal(1.0 + decay(factor, inner_prod), approx=True)
        use(product(weight, others))


def join(visitors, joined):
    if len(visitors) == 1:
        return visitors[0]
    start = 0
    for visitor in visitors:
        joined[pl.ds(start, visitor.shape[0])] = visitor[...]
        start += visitor.shape[0]
    return joined.at[pl.ds(0, start)]


def pick_kernel(image_ref, text_ref, image_head, text_head, far_own, near_own, sems):
    def move(k, source, out):
        return pltpu.make_async_copy(source.at[pl.ds(0, out.shape[0])], out, sems.at[k])

    heads = [move(0, image_ref, image_head), move(1, text_ref, text_head)]
    for head in heads:
        head.start()
    for is_core, (far, near) in enumerate(((image_ref, text_ref), (text_ref, image_ref))):

        @pl.when(core() == is_core)
        def _():
            blocks = [move(2, far, far_own), move(3, near, near_own)]
            for block in blocks:
                block.start()
            for block in blocks:
                block.wait()

    for head in heads:
        head.wait()


def own_kernel(factor, image_ref, text_ref, near_own, *refs):
    near, (image_sum, text_sum, joined) = refs[:NEAR_PARTS], refs[NEAR_PARTS:]
    rows = image_ref.shape[0]
    shape = (rows, rows)
    matched = lax.broadcasted_iota(jnp.int32, shape, 0) == lax.broadcasted_iota(
        jnp.int32, shape, 1
    )
    for own, others, total in ((image_ref, text_ref, image_sum), (text_ref, image_ref, text_sum)):
        chance = 1.0 / (1.0 + decay(factor, logits(own, others)))
        total[...] = product(chance - matched.astype(jnp.float32), others)
    is_1 = core().astype(jnp.float32)

    def use(value):
        image_sum[...] += value * is_1
        text_sum[...] += value * (1.0 - is_1)

    add_all(factor, [(near_own, join(near, joined), use)])


def step_kernel(factor, units, sides, *refs):
    is_1 = core().astype(jnp.float32)
    parts = []
    for _, count in units:
        parts.append((refs[0], refs[1 : 1 + count]))
        refs = refs[1 + count :]
    totals = dict(zip(sides, refs))
    sums = dict(zip(sides, refs[len(sides) :]))
    joined = refs[2 * len(sides) :]
    touched = set()

    def add(side, value):
        sums[side][...] = (sums if side in touched else totals)[side][...] + value
        touched.add(side)

    def use(side, value):
        if side < 2:
            add(side, value)
        else:
            add(side - 2, value * (1.0 - is_1))
            add(3 - side, value * is_1)

    add_all(
        factor,
        [
            (own, join(visitors, scratch), functools.partial(use, side))
            for (side, _), (own, visitors), scratch in zip(units, parts, joined)
        ],
    )


def last_kernel(factor, far_own, near_own, far, texts, images, *refs):
    sums, outs, (helds, joined, others, sems) = refs[:2], refs[2:4], refs[4:]
    rows = far_own.shape[0]
    visitors = (texts, images)

    def on_each_core(act):
        for is_core in (0, 1):
            pl.when(core() == is_core)(functools.partial(act, is_core))

    def move(is_far, side, first):
        span = pl.ds(first, COPY_ROWS)
        sem = sems.at[is_far, first // COPY_ROWS]
        return pltpu.make_async_copy(helds.at[is_far, span], outs[side].at[span], sem)

    def place(side):
        joined[pl.ds(rows, texts.shape[0])] = visitors[side][...]
        others[...] = visitors[1 - side][...]

    def use(is_far, start, value):
        def add(far_side):
            side = far_side if is_far else 1 - far_side
            span = pl.ds(start, LAST_TILE)
            helds[is_far, span] = (sums[side][span] + value) * factor
            for first in range(start, start + LAST_TILE, COPY_ROWS):
                move(is_far, side, first).start()

        on_each_core(add)

    def finish(far_side):
        for is_far in (0, 1):
            for first in range(0, rows, COPY_ROWS):
                move(is_far, far_side if is_far else 1 - far_side, first).wait()

    joined[pl.ds(0, rows)] = far[...]
    on_each_core(place)
    units = []
    for is_far, (own, met) in enumerate(((near_own, others), (far_own, joined))):
        for start in range(0, rows, LAST_TILE):
            act = functools.partial(use, is_far, start)
            units.append((own.at[pl.ds(start, LAST_TILE)], met, act))
    add_all(factor, units)
    on_each_core(finish)


def local(image_embed, text_embed):
    rows, width = image_embed.shape
    dtype = image_embed.dtype
    factor = 2.0 / math.sqrt(width)
    kept = pltpu.VMEM((rows, width), jnp.float32)
    block = pltpu.VMEM((rows, width), dtype)
    grad = jax.ShapeDtypeStruct((rows, width), jnp.float32)

    def call(kernel, outs, operands, scratch=(), aliases=None, in_spec=VMEM):
        return pl.pallas_call(
            kernel,
            out_shape=tuple(outs),
            in_specs=[in_spec] * len(operands),
            out_specs=(ANY if outs[0] is grad else VMEM,) * len(outs),
            scratch_shapes=list(scratch),
            input_output_aliases=aliases or {},
            cost_estimate=pl.CostEstimate(flops=1, bytes_accessed=1, transcendentals=0),
            compiler_params=pltpu.CompilerParams(vmem_limit_bytes=VMEM_MIB << 20),
        )(*operands)

    def depth(visitors):
        return pltpu.VMEM((sum(visitor.shape[0] for visitor in visitors), width), dtype)

    def step(units, sums):
        sides = tuple(sums)
        operands = [ref for _, own, visitors in units for ref in (own, *visitors)]
        counts = [(side, len(visitors)) for side, _, visitors in units]
        return dict(
            zip(
                sides,
                call(
                    functools.partial(step_kernel, factor, counts, sides),
                    [kept] * len(sides),
                    (*operands, *sums.values()),
                    [depth(visitors) for _, _, visitors in units],
                    {len(operands) + k: k for k in range(len(sides))},
                ),
            )
        )

    def after(value, *earlier):
        return lax.optimization_barrier((value, *earlier))[0]

    def next_images(piece):
        return send(piece, lambda i: i - 2)

    def next_texts(piece):
        return send(piece, lambda i: i + 2)

    in_hbm = [pltpu.with_memory_space_constraint(x, pltpu.HBM) for x in (image_embed, text_embed)]
    cut_images, cut_texts = rows * FIRST_IMAGES // 16, rows * FIRST_TEXTS // 16
    heads = (cut_images, cut_texts)
    image_head, text_head, far_own, near_own = call(
        pick_kernel,
        [pltpu.VMEM((head, width), dtype) for head in heads] + [block, block],
        in_hbm,
        [pltpu.SemaphoreType.DMA((4,))],
        in_spec=ANY,
    )
    images, texts = next_images(image_head), next_texts(text_head)
    far = send(far_own, lambda i: i + 3 if i % 2 else i - 3)
    near = swap(near_own, 1)
    later_images = next_images(image_embed[cut_images:])
    later_texts = next_texts(text_embed[cut_texts:])
    sums = call(
        functools.partial(own_kernel, factor),
        (kept, kept),
        (image_embed, text_embed, near_own, *near),
        [block],
    )
    sums = dict(enumerate(sums))

    images, texts = after(images, *sums.values()), after(texts, *sums.values())
    swapped_images, swapped_texts = swap(images, 2), swap(texts, 2)
    sums = step(
        [
            (0, image_embed, (texts, *swapped_texts)),
            (1, text_embed, (images, *swapped_images)),
        ],
        sums,
    )

    images, texts = after(later_images, sums[0]), after(later_texts, sums[0])
    swapped_images, swapped_texts = swap(images, 1), swap(texts, 1)
    sums = step(
        [
            (0, image_embed, (texts,)),
            (1, text_embed, (images,)),
        ],
        sums,
    )
    return call(
        functools.partial(last_kernel, factor),
        (grad, grad),
        (far_own, near_own, far, *swapped_texts, *swapped_images, sums[0], sums[1]),
        [
            pltpu.VMEM((2, rows, width), jnp.float32),
            pltpu.VMEM((2 * rows - cut_texts, width), dtype),
            pltpu.VMEM((rows - cut_texts, width), dtype),
            pltpu.SemaphoreType.DMA((2, rows // COPY_ROWS)),
        ],
    )


def solution(mesh):
    spec = P(("rep", "blk"), None)
    return jax.shard_map(
        local, mesh=mesh, in_specs=(spec, spec), out_specs=(spec, spec), check_vma=False
    )
```

```python
import functools
import math

import jax
import jax.numpy as jnp
from jax import lax
from jax.experimental import pallas as pl
from jax.experimental.pallas import tpu as pltpu
from jax.sharding import PartitionSpec as P

AXIS = "blk"
FIRST_IMAGES = 8
FIRST_TEXTS = 8
NEAR_PARTS = 1
LAST_TILE = 256
COPY_ROWS = 128
VMEM_MIB = 32
VMEM = pl.BlockSpec(memory_space=pltpu.VMEM)
ANY = pl.BlockSpec(memory_space=pl.ANY)
LOG2_E = math.log2(math.e)


def send(block, target):
    count = lax.axis_size(AXIS)
    return lax.ppermute(block, AXIS, [(i, target(i) % count) for i in range(count)])


def swap(block, parts):
    return [send(part, lambda i: i ^ 1) for part in jnp.split(block, parts)]


def core():
    return lax.rem(lax.axis_index(AXIS), 2)


def logits(own, others):
    return lax.dot_general(
        own[...], others[...], (((1,), (1,)), ((), ())), preferred_element_type=jnp.float32
    )


def decay(factor, inner_prod):
    return jnp.exp2(LOG2_E - (factor * LOG2_E) * inner_prod)


def product(weight, others):
    return jnp.dot(weight.astype(jnp.bfloat16), others[...], preferred_element_type=jnp.float32)


def add_all(factor, units):
    following = logits(*units[0][:2])
    for k, (_, others, use) in enumerate(units):
        inner_prod = following
        if k + 1 < len(units):
            following = logits(*units[k + 1][:2])
        weight = pl.reciprocal(1.0 + decay(factor, inner_prod), approx=True)
        use(product(weight, others))


def join(visitors, joined):
    if len(visitors) == 1:
        return visitors[0]
    start = 0
    for visitor in visitors:
        joined[pl.ds(start, visitor.shape[0])] = visitor[...]
        start += visitor.shape[0]
    return joined.at[pl.ds(0, start)]


def pick_kernel(image_ref, text_ref, image_head, text_head, far_own, near_own, sems):
    def move(k, source, out):
        return pltpu.make_async_copy(source.at[pl.ds(0, out.shape[0])], out, sems.at[k])

    heads = [move(0, image_ref, image_head), move(1, text_ref, text_head)]
    for head in heads:
        head.start()
    for is_core, (far, near) in enumerate(((image_ref, text_ref), (text_ref, image_ref))):

        @pl.when(core() == is_core)
        def _():
            blocks = [move(2, far, far_own), move(3, near, near_own)]
            for block in blocks:
                block.start()
            for block in blocks:
                block.wait()

    for head in heads:
        head.wait()


def own_kernel(factor, image_ref, text_ref, near_own, *refs):
    near, (image_sum, text_sum, joined) = refs[:NEAR_PARTS], refs[NEAR_PARTS:]
    rows = image_ref.shape[0]
    shape = (rows, rows)
    matched = lax.broadcasted_iota(jnp.int32, shape, 0) == lax.broadcasted_iota(
        jnp.int32, shape, 1
    )
    for own, others, total in ((image_ref, text_ref, image_sum), (text_ref, image_ref, text_sum)):
        chance = 1.0 / (1.0 + decay(factor, logits(own, others)))
        total[...] = product(chance - matched.astype(jnp.float32), others)
    is_1 = core().astype(jnp.float32)

    def use(value):
        image_sum[...] += value * is_1
        text_sum[...] += value * (1.0 - is_1)

    add_all(factor, [(near_own, join(near, joined), use)])


def step_kernel(factor, units, sides, *refs):
    is_1 = core().astype(jnp.float32)
    parts = []
    for _, count in units:
        parts.append((refs[0], refs[1 : 1 + count]))
        refs = refs[1 + count :]
    totals = dict(zip(sides, refs))
    sums = dict(zip(sides, refs[len(sides) :]))
    joined = refs[2 * len(sides) :]
    touched = set()

    def add(side, value):
        sums[side][...] = (sums if side in touched else totals)[side][...] + value
        touched.add(side)

    def use(side, value):
        if side < 2:
            add(side, value)
        else:
            add(side - 2, value * (1.0 - is_1))
            add(3 - side, value * is_1)

    add_all(
        factor,
        [
            (own, join(visitors, scratch), functools.partial(use, side))
            for (side, _), (own, visitors), scratch in zip(units, parts, joined)
        ],
    )


def last_kernel(factor, counts, far_own, far, *refs):
    parts = []
    for count in counts:
        parts.append((refs[0], refs[1 : 1 + count], refs[1 + count]))
        refs = refs[2 + count :]
    outs, helds, joined, sems = refs[:2], refs[2:4], refs[4:6], refs[6]
    starts = range(0, far_own.shape[0], LAST_TILE)
    is_1 = core().astype(jnp.float32)
    copies = []

    def use_far(start, value):
        rows = pl.ds(start, LAST_TILE)
        helds[0][rows] = parts[0][2][rows] + value * (1.0 - is_1)
        helds[1][rows] = parts[1][2][rows] + value * is_1

    def use(held, out, start, value):
        rows = pl.ds(start, LAST_TILE)
        held[rows] = (held[rows] + value) * factor
        for first in range(start, start + LAST_TILE, COPY_ROWS):
            span = pl.ds(first, COPY_ROWS)
            copies.append(pltpu.make_async_copy(held.at[span], out.at[span], sems.at[len(copies)]))
            copies[-1].start()

    def unit(own, others, start, act, *args):
        return (own.at[pl.ds(start, LAST_TILE)], others, functools.partial(act, *args, start))

    units = [unit(far_own, far, start, use_far) for start in starts]
    for (own, visitors, _), held, out, scratch in zip(parts, helds, outs, joined):
        others = join(visitors, scratch)
        units += [unit(own, others, start, use, held, out) for start in starts]
    add_all(factor, units)
    for copy in copies:
        copy.wait()


def local(image_embed, text_embed):
    rows, width = image_embed.shape
    dtype = image_embed.dtype
    factor = 2.0 / math.sqrt(width)
    kept = pltpu.VMEM((rows, width), jnp.float32)
    block = pltpu.VMEM((rows, width), dtype)
    grad = jax.ShapeDtypeStruct((rows, width), jnp.float32)

    def call(kernel, outs, operands, scratch=(), aliases=None, in_spec=VMEM):
        return pl.pallas_call(
            kernel,
            out_shape=tuple(outs),
            in_specs=[in_spec] * len(operands),
            out_specs=(ANY if outs[0] is grad else VMEM,) * len(outs),
            scratch_shapes=list(scratch),
            input_output_aliases=aliases or {},
            cost_estimate=pl.CostEstimate(flops=1, bytes_accessed=1, transcendentals=0),
            compiler_params=pltpu.CompilerParams(vmem_limit_bytes=VMEM_MIB << 20),
        )(*operands)

    def depth(visitors):
        return pltpu.VMEM((sum(visitor.shape[0] for visitor in visitors), width), dtype)

    def step(units, sums):
        sides = tuple(sums)
        operands = [ref for _, own, visitors in units for ref in (own, *visitors)]
        counts = [(side, len(visitors)) for side, _, visitors in units]
        return dict(
            zip(
                sides,
                call(
                    functools.partial(step_kernel, factor, counts, sides),
                    [kept] * len(sides),
                    (*operands, *sums.values()),
                    [depth(visitors) for _, _, visitors in units],
                    {len(operands) + k: k for k in range(len(sides))},
                ),
            )
        )

    def after(value, *earlier):
        return lax.optimization_barrier((value, *earlier))[0]

    def next_images(piece):
        return send(piece, lambda i: i - 2)

    def next_texts(piece):
        return send(piece, lambda i: i + 2)

    in_hbm = [pltpu.with_memory_space_constraint(x, pltpu.HBM) for x in (image_embed, text_embed)]
    cut_images, cut_texts = rows * FIRST_IMAGES // 16, rows * FIRST_TEXTS // 16
    heads = (cut_images, cut_texts)
    image_head, text_head, far_own, near_own = call(
        pick_kernel,
        [pltpu.VMEM((head, width), dtype) for head in heads] + [block, block],
        in_hbm,
        [pltpu.SemaphoreType.DMA((4,))],
        in_spec=ANY,
    )
    images, texts = next_images(image_head), next_texts(text_head)
    far = send(far_own, lambda i: i + 3 if i % 2 else i - 3)
    near = swap(near_own, 1)
    later_images = next_images(image_embed[cut_images:])
    later_texts = next_texts(text_embed[cut_texts:])
    sums = call(
        functools.partial(own_kernel, factor),
        (kept, kept),
        (image_embed, text_embed, near_own, *near),
        [block],
    )
    sums = dict(enumerate(sums))

    images, texts = after(images, *sums.values()), after(texts, *sums.values())
    swapped_images, swapped_texts = swap(images, 2), swap(texts, 2)
    sums = step(
        [
            (1, text_embed, (images, *swapped_images)),
            (0, image_embed, (texts, *swapped_texts)),
        ],
        sums,
    )

    images, texts = after(later_images, sums[0]), after(later_texts, sums[0])
    swapped_images, swapped_texts = swap(images, 1), swap(texts, 1)
    sums = step(
        [
            (0, image_embed, (texts,)),
            (1, text_embed, (images,)),
        ],
        sums,
    )
    operands = (image_embed, *swapped_texts, sums[0], text_embed, *swapped_images, sums[1])
    operands = (far_own, far, *operands)
    return call(
        functools.partial(last_kernel, factor, (1, 1)),
        (grad, grad),
        operands,
        [kept, kept, depth((texts,)), depth((images,))]
        + [pltpu.SemaphoreType.DMA((2 * rows // COPY_ROWS,))],
    )


def solution(mesh):
    spec = P(("rep", "blk"), None)
    return jax.shard_map(
        local, mesh=mesh, in_specs=(spec, spec), out_specs=(spec, spec), check_vma=False
    )
```

```python
import functools
import math

import jax
import jax.numpy as jnp
from jax import lax
from jax.experimental import pallas as pl
from jax.experimental.pallas import tpu as pltpu
from jax.sharding import PartitionSpec as P

AXIS = "blk"
FIRST_IMAGES = 8
FIRST_TEXTS = 8
NEAR_ENDS = (11, 22)
NEAR_PARTS = len(NEAR_ENDS) + 1
LAST_TILE = 256
COPY_ROWS = 128
VMEM_MIB = 32
VMEM = pl.BlockSpec(memory_space=pltpu.VMEM)
ANY = pl.BlockSpec(memory_space=pl.ANY)
LOG2_E = math.log2(math.e)


def send(block, target):
    count = lax.axis_size(AXIS)
    return lax.ppermute(block, AXIS, [(i, target(i) % count) for i in range(count)])


def swap(block, parts):
    return [send(part, lambda i: i ^ 1) for part in jnp.split(block, parts)]


def core():
    return lax.rem(lax.axis_index(AXIS), 2)


def logits(own, others):
    return lax.dot_general(
        own[...], others[...], (((1,), (1,)), ((), ())), preferred_element_type=jnp.float32
    )


def decay(factor, inner_prod):
    return jnp.exp2(LOG2_E - (factor * LOG2_E) * inner_prod)


def product(weight, others):
    return jnp.dot(weight.astype(jnp.bfloat16), others[...], preferred_element_type=jnp.float32)


def add_all(factor, units):
    following = logits(*units[0][:2])
    for k, (_, others, use) in enumerate(units):
        inner_prod = following
        if k + 1 < len(units):
            following = logits(*units[k + 1][:2])
        weight = pl.reciprocal(1.0 + decay(factor, inner_prod), approx=True)
        use(product(weight, others))


def join(visitors, joined):
    if len(visitors) == 1:
        return visitors[0]
    start = 0
    for visitor in visitors:
        joined[pl.ds(start, visitor.shape[0])] = visitor[...]
        start += visitor.shape[0]
    return joined.at[pl.ds(0, start)]


def pick_kernel(image_ref, text_ref, *refs):
    outs, sems = refs[:2], refs[2]
    copies = []
    for k, (source, out) in enumerate(zip((image_ref, text_ref), outs)):
        rows = pl.ds(0, out.shape[0])
        copies.append(pltpu.make_async_copy(source.at[rows], out, sems.at[k]))
        copies[-1].start()
    for copy in copies:
        copy.wait()


def core_pick_kernel(image_ref, text_ref, far_own, near_own, sems):
    for is_core, (far, near) in enumerate(((image_ref, text_ref), (text_ref, image_ref))):

        @pl.when(core() == is_core)
        def _():
            copies = [
                pltpu.make_async_copy(far, far_own, sems.at[0]),
                pltpu.make_async_copy(near, near_own, sems.at[1]),
            ]
            for copy in copies:
                copy.start()
            for copy in copies:
                copy.wait()


def own_kernel(factor, image_ref, text_ref, near_own, *refs):
    near, (image_sum, text_sum, joined) = refs[:NEAR_PARTS], refs[NEAR_PARTS:]
    rows = image_ref.shape[0]
    shape = (rows, rows)
    matched = lax.broadcasted_iota(jnp.int32, shape, 0) == lax.broadcasted_iota(
        jnp.int32, shape, 1
    )
    for own, others, total in ((image_ref, text_ref, image_sum), (text_ref, image_ref, text_sum)):
        chance = 1.0 / (1.0 + decay(factor, logits(own, others)))
        total[...] = product(chance - matched.astype(jnp.float32), others)
    is_1 = core().astype(jnp.float32)

    def use(value):
        image_sum[...] += value * is_1
        text_sum[...] += value * (1.0 - is_1)

    add_all(factor, [(near_own, join(near, joined), use)])


def step_kernel(factor, units, sides, *refs):
    is_1 = core().astype(jnp.float32)
    parts = []
    for _, count in units:
        parts.append((refs[0], refs[1 : 1 + count]))
        refs = refs[1 + count :]
    totals = dict(zip(sides, refs))
    sums = dict(zip(sides, refs[len(sides) :]))
    joined = refs[2 * len(sides) :]
    touched = set()

    def add(side, value):
        sums[side][...] = (sums if side in touched else totals)[side][...] + value
        touched.add(side)

    def use(side, value):
        if side < 2:
            add(side, value)
        else:
            add(side - 2, value * (1.0 - is_1))
            add(3 - side, value * is_1)

    add_all(
        factor,
        [
            (own, join(visitors, scratch), functools.partial(use, side))
            for (side, _), (own, visitors), scratch in zip(units, parts, joined)
        ],
    )


def last_kernel(factor, far_own, far, image_ref, texts, image_sum, text_ref, images, *refs):
    text_sum, outs, helds, far_held, sems = refs[0], refs[1:3], refs[3:5], refs[5], refs[6]
    sides = ((image_ref, texts, image_sum), (text_ref, images, text_sum))
    is_1 = core().astype(jnp.float32)
    masks = ((1.0 - is_1) * factor, is_1 * factor)
    copies = []

    def use_far(start, value):
        far_held[pl.ds(start, LAST_TILE)] = value

    def use(side, start, value):
        rows = pl.ds(start, LAST_TILE)
        held, out = helds[side], outs[side]
        total = (sides[side][2][rows] + value) * factor
        held[rows] = total + far_held[rows] * masks[side]
        for first in range(start, start + LAST_TILE, COPY_ROWS):
            span = pl.ds(first, COPY_ROWS)
            copies.append(pltpu.make_async_copy(held.at[span], out.at[span], sems.at[len(copies)]))
            copies[-1].start()

    units = []
    for start in range(0, far_own.shape[0], LAST_TILE):
        rows = pl.ds(start, LAST_TILE)
        units.append((far_own.at[rows], far, functools.partial(use_far, start)))
        for side, (own, others, _) in enumerate(sides):
            units.append((own.at[rows], others, functools.partial(use, side, start)))
    add_all(factor, units)
    for copy in copies:
        copy.wait()


def local(image_embed, text_embed):
    rows, width = image_embed.shape
    dtype = image_embed.dtype
    factor = 2.0 / math.sqrt(width)
    kept = pltpu.VMEM((rows, width), jnp.float32)
    block = pltpu.VMEM((rows, width), dtype)
    grad = jax.ShapeDtypeStruct((rows, width), jnp.float32)

    def call(kernel, outs, operands, scratch=(), aliases=None, in_spec=VMEM):
        return pl.pallas_call(
            kernel,
            out_shape=tuple(outs),
            in_specs=[in_spec] * len(operands),
            out_specs=(ANY if outs[0] is grad else VMEM,) * len(outs),
            scratch_shapes=list(scratch),
            input_output_aliases=aliases or {},
            cost_estimate=pl.CostEstimate(flops=1, bytes_accessed=1, transcendentals=0),
            compiler_params=pltpu.CompilerParams(vmem_limit_bytes=VMEM_MIB << 20),
        )(*operands)

    def depth(visitors):
        return pltpu.VMEM((sum(visitor.shape[0] for visitor in visitors), width), dtype)

    def step(units, sums):
        sides = tuple(sums)
        operands = [ref for _, own, visitors in units for ref in (own, *visitors)]
        counts = [(side, len(visitors)) for side, _, visitors in units]
        return dict(
            zip(
                sides,
                call(
                    functools.partial(step_kernel, factor, counts, sides),
                    [kept] * len(sides),
                    (*operands, *sums.values()),
                    [depth(visitors) for _, _, visitors in units],
                    {len(operands) + k: k for k in range(len(sides))},
                ),
            )
        )

    def after(value, *earlier):
        return lax.optimization_barrier((value, *earlier))[0]

    def next_images(piece):
        return send(piece, lambda i: i - 2)

    def next_texts(piece):
        return send(piece, lambda i: i + 2)

    in_hbm = [pltpu.with_memory_space_constraint(x, pltpu.HBM) for x in (image_embed, text_embed)]
    cut_images, cut_texts = rows * FIRST_IMAGES // 16, rows * FIRST_TEXTS // 16
    heads = (cut_images, cut_texts)
    image_head, text_head = call(
        pick_kernel,
        [pltpu.VMEM((head, width), dtype) for head in heads],
        in_hbm,
        [pltpu.SemaphoreType.DMA((2,))],
        in_spec=ANY,
    )
    images, texts = next_images(image_head), next_texts(text_head)
    far_own, near_own = call(
        core_pick_kernel, [block, block], in_hbm, [pltpu.SemaphoreType.DMA((2,))], in_spec=ANY
    )
    far = send(far_own, lambda i: i + 3 if i % 2 else i - 3)
    near = [
        send(part, lambda i: i ^ 1)
        for part in jnp.split(near_own, [rows * end // 32 for end in NEAR_ENDS])
    ]
    later_images = next_images(image_embed[cut_images:])
    later_texts = next_texts(text_embed[cut_texts:])
    sums = call(
        functools.partial(own_kernel, factor),
        (kept, kept),
        (image_embed, text_embed, near_own, *near),
        [block],
    )
    sums = dict(enumerate(sums))

    images, texts = after(images, *sums.values()), after(texts, *sums.values())
    swapped_images, swapped_texts = swap(images, 2), swap(texts, 2)
    sums = step(
        [
            (1, text_embed, (images, *swapped_images)),
            (0, image_embed, (texts, *swapped_texts)),
        ],
        sums,
    )

    images, texts = after(later_images, sums[0]), after(later_texts, sums[0])
    swapped_images, swapped_texts = swap(images, 1), swap(texts, 1)
    sums = step(
        [
            (0, image_embed, (texts,)),
            (1, text_embed, (images,)),
        ],
        sums,
    )
    return call(
        functools.partial(last_kernel, factor),
        (grad, grad),
        (far_own, far, image_embed, *swapped_texts, sums[0], text_embed, *swapped_images, sums[1]),
        [kept] * 3 + [pltpu.SemaphoreType.DMA((2 * rows // COPY_ROWS,))],
    )


def solution(mesh):
    spec = P(("rep", "blk"), None)
    return jax.shard_map(
        local, mesh=mesh, in_specs=(spec, spec), out_specs=(spec, spec), check_vma=False
    )
```

```python
import functools
import math

import jax
import jax.numpy as jnp
from jax import lax
from jax.experimental import pallas as pl
from jax.experimental.pallas import tpu as pltpu
from jax.sharding import PartitionSpec as P

AXIS = "blk"
NEAR_PARTS = 2
LAST_TILE = 256
COPY_ROWS = 128
VMEM_MIB = 32
VMEM = pl.BlockSpec(memory_space=pltpu.VMEM)
ANY = pl.BlockSpec(memory_space=pl.ANY)
LOG2_E = math.log2(math.e)


def send(block, target):
    count = lax.axis_size(AXIS)
    return lax.ppermute(block, AXIS, [(i, target(i) % count) for i in range(count)])


def swap(block, parts):
    return [send(part, lambda i: i ^ 1) for part in jnp.split(block, parts)]


def core():
    return lax.rem(lax.axis_index(AXIS), 2)


def logits(own, others):
    return lax.dot_general(
        own[...], others[...], (((1,), (1,)), ((), ())), preferred_element_type=jnp.float32
    )


def decay(factor, inner_prod):
    return jnp.exp2(LOG2_E - (factor * LOG2_E) * inner_prod)


def product(weight, others):
    return jnp.dot(weight.astype(jnp.bfloat16), others[...], preferred_element_type=jnp.float32)


def add_all(factor, units):
    following = logits(*units[0][:2])
    for k, (_, others, use) in enumerate(units):
        inner_prod = following
        if k + 1 < len(units):
            following = logits(*units[k + 1][:2])
        weight = pl.reciprocal(1.0 + decay(factor, inner_prod), approx=True)
        use(product(weight, others))


def join(visitors, joined):
    if len(visitors) == 1:
        return visitors[0]
    start = 0
    for visitor in visitors:
        joined[pl.ds(start, visitor.shape[0])] = visitor[...]
        start += visitor.shape[0]
    return joined.at[pl.ds(0, start)]


def core_pick_kernel(image_ref, text_ref, far_own, near_own, sems):
    for is_core, (far, near) in enumerate(((image_ref, text_ref), (text_ref, image_ref))):

        @pl.when(core() == is_core)
        def _():
            copies = [
                pltpu.make_async_copy(far, far_own, sems.at[0]),
                pltpu.make_async_copy(near, near_own, sems.at[1]),
            ]
            for copy in copies:
                copy.start()
            for copy in copies:
                copy.wait()


def own_kernel(factor, image_ref, text_ref, near_own, *refs):
    near, (image_sum, text_sum, joined) = refs[:NEAR_PARTS], refs[NEAR_PARTS:]
    rows = image_ref.shape[0]
    shape = (rows, rows)
    matched = lax.broadcasted_iota(jnp.int32, shape, 0) == lax.broadcasted_iota(
        jnp.int32, shape, 1
    )
    for own, others, total in ((image_ref, text_ref, image_sum), (text_ref, image_ref, text_sum)):
        chance = 1.0 / (1.0 + decay(factor, logits(own, others)))
        total[...] = product(chance - matched.astype(jnp.float32), others)
    is_1 = core().astype(jnp.float32)

    def use(value):
        image_sum[...] += value * is_1
        text_sum[...] += value * (1.0 - is_1)

    add_all(factor, [(near_own, join(near, joined), use)])


def step_kernel(factor, units, sides, *refs):
    is_1 = core().astype(jnp.float32)
    parts = []
    for _, count in units:
        parts.append((refs[0], refs[1 : 1 + count]))
        refs = refs[1 + count :]
    totals = dict(zip(sides, refs))
    sums = dict(zip(sides, refs[len(sides) :]))
    joined = refs[2 * len(sides) :]
    touched = set()

    def add(side, value):
        sums[side][...] = (sums if side in touched else totals)[side][...] + value
        touched.add(side)

    def use(side, value):
        if side < 2:
            add(side, value)
        else:
            add(side - 2, value * (1.0 - is_1))
            add(3 - side, value * is_1)

    add_all(
        factor,
        [
            (own, join(visitors, scratch), functools.partial(use, side))
            for (side, _), (own, visitors), scratch in zip(units, parts, joined)
        ],
    )


def last_kernel(factor, counts, far_own, far, *refs):
    parts = []
    for count in counts:
        parts.append((refs[0], refs[1 : 1 + count], refs[1 + count]))
        refs = refs[2 + count :]
    outs, helds, joined, sems = refs[:2], refs[2:4], refs[4:6], refs[6]
    starts = range(0, far_own.shape[0], LAST_TILE)
    is_1 = core().astype(jnp.float32)
    copies = []

    def use_far(start, value):
        rows = pl.ds(start, LAST_TILE)
        helds[0][rows] = parts[0][2][rows] + value * (1.0 - is_1)
        helds[1][rows] = parts[1][2][rows] + value * is_1

    def use(held, out, start, value):
        rows = pl.ds(start, LAST_TILE)
        held[rows] = (held[rows] + value) * factor
        for first in range(start, start + LAST_TILE, COPY_ROWS):
            span = pl.ds(first, COPY_ROWS)
            copies.append(pltpu.make_async_copy(held.at[span], out.at[span], sems.at[len(copies)]))
            copies[-1].start()

    def unit(own, others, start, act, *args):
        return (own.at[pl.ds(start, LAST_TILE)], others, functools.partial(act, *args, start))

    units = [unit(far_own, far, start, use_far) for start in starts]
    for (own, visitors, _), held, out, scratch in zip(parts, helds, outs, joined):
        others = join(visitors, scratch)
        units += [unit(own, others, start, use, held, out) for start in starts]
    add_all(factor, units)
    for copy in copies:
        copy.wait()


def local(image_embed, text_embed):
    rows, width = image_embed.shape
    dtype = image_embed.dtype
    factor = 2.0 / math.sqrt(width)
    kept = pltpu.VMEM((rows, width), jnp.float32)
    block = pltpu.VMEM((rows, width), dtype)
    grad = jax.ShapeDtypeStruct((rows, width), jnp.float32)

    def call(kernel, outs, operands, scratch=(), aliases=None, in_spec=VMEM):
        return pl.pallas_call(
            kernel,
            out_shape=tuple(outs),
            in_specs=[in_spec] * len(operands),
            out_specs=(ANY if outs[0] is grad else VMEM,) * len(outs),
            scratch_shapes=list(scratch),
            input_output_aliases=aliases or {},
            cost_estimate=pl.CostEstimate(flops=1, bytes_accessed=1, transcendentals=0),
            compiler_params=pltpu.CompilerParams(vmem_limit_bytes=VMEM_MIB << 20),
        )(*operands)

    def depth(visitors):
        return pltpu.VMEM((sum(visitor.shape[0] for visitor in visitors), width), dtype)

    def step(units, sums):
        sides = tuple(sums)
        operands = [ref for _, own, visitors in units for ref in (own, *visitors)]
        counts = [(side, len(visitors)) for side, _, visitors in units]
        return dict(
            zip(
                sides,
                call(
                    functools.partial(step_kernel, factor, counts, sides),
                    [kept] * len(sides),
                    (*operands, *sums.values()),
                    [depth(visitors) for _, _, visitors in units],
                    {len(operands) + k: k for k in range(len(sides))},
                ),
            )
        )

    def after(value, *earlier):
        return lax.optimization_barrier((value, *earlier))[0]

    def next_images(piece):
        return send(piece, lambda i: i - 2)

    def next_texts(piece):
        return send(piece, lambda i: i + 2)

    in_hbm = [pltpu.with_memory_space_constraint(x, pltpu.HBM) for x in (image_embed, text_embed)]
    images, texts = next_images(image_embed), next_texts(text_embed)
    far_own, near_own = call(
        core_pick_kernel, [block, block], in_hbm, [pltpu.SemaphoreType.DMA((2,))], in_spec=ANY
    )
    far = send(far_own, lambda i: i + 3 if i % 2 else i - 3)
    near = swap(near_own, 2)
    sums = call(
        functools.partial(own_kernel, factor),
        (kept, kept),
        (image_embed, text_embed, near_own, *near),
        [block],
    )
    sums = dict(enumerate(sums))

    images, texts = after(images, *sums.values()), after(texts, *sums.values())
    swapped_images, swapped_texts = swap(images, 2), swap(texts, 1)
    sums = step([(1, text_embed, (images,)), (0, image_embed, (texts,))], sums)
    operands = (image_embed, *swapped_texts, sums[0], text_embed, *swapped_images, sums[1])
    operands = (far_own, far, *operands)
    return call(
        functools.partial(last_kernel, factor, (1, 2)),
        (grad, grad),
        operands,
        [kept, kept, depth((texts,)), depth((images,))]
        + [pltpu.SemaphoreType.DMA((2 * rows // COPY_ROWS,))],
    )


def solution(mesh):
    spec = P(("rep", "blk"), None)
    return jax.shard_map(
        local, mesh=mesh, in_specs=(spec, spec), out_specs=(spec, spec), check_vma=False
    )
```

```python
import functools
import math

import jax
import jax.numpy as jnp
from jax import lax
from jax.experimental import pallas as pl
from jax.experimental.pallas import tpu as pltpu
from jax.sharding import PartitionSpec as P

AXIS = "blk"
NEAR_PARTS = 2
LAST_TILE = 256
COPY_ROWS = 128
VMEM_MIB = 32
VMEM = pl.BlockSpec(memory_space=pltpu.VMEM)
ANY = pl.BlockSpec(memory_space=pl.ANY)
LOG2_E = math.log2(math.e)


def send(block, target):
    count = lax.axis_size(AXIS)
    return lax.ppermute(block, AXIS, [(i, target(i) % count) for i in range(count)])


def swap(block, parts):
    return [send(part, lambda i: i ^ 1) for part in jnp.split(block, parts)]


def core():
    return lax.rem(lax.axis_index(AXIS), 2)


def logits(own, others):
    return lax.dot_general(
        own[...], others[...], (((1,), (1,)), ((), ())), preferred_element_type=jnp.float32
    )


def decay(factor, inner_prod):
    return jnp.exp2(LOG2_E - (factor * LOG2_E) * inner_prod)


def product(weight, others):
    return jnp.dot(weight.astype(jnp.bfloat16), others[...], preferred_element_type=jnp.float32)


def add_all(factor, units):
    following = logits(*units[0][:2])
    for k, (_, others, use) in enumerate(units):
        inner_prod = following
        if k + 1 < len(units):
            following = logits(*units[k + 1][:2])
        weight = pl.reciprocal(1.0 + decay(factor, inner_prod), approx=True)
        use(product(weight, others))


def join(visitors, joined):
    if len(visitors) == 1:
        return visitors[0]
    start = 0
    for visitor in visitors:
        joined[pl.ds(start, visitor.shape[0])] = visitor[...]
        start += visitor.shape[0]
    return joined.at[pl.ds(0, start)]


def core_pick_kernel(image_ref, text_ref, far_own, near_own, sems):
    for is_core, (far, near) in enumerate(((image_ref, text_ref), (text_ref, image_ref))):

        @pl.when(core() == is_core)
        def _():
            copies = [
                pltpu.make_async_copy(far, far_own, sems.at[0]),
                pltpu.make_async_copy(near, near_own, sems.at[1]),
            ]
            for copy in copies:
                copy.start()
            for copy in copies:
                copy.wait()


def own_kernel(factor, image_ref, text_ref, near_own, *refs):
    near, (image_sum, text_sum, joined) = refs[:NEAR_PARTS], refs[NEAR_PARTS:]
    rows = image_ref.shape[0]
    shape = (rows, rows)
    matched = lax.broadcasted_iota(jnp.int32, shape, 0) == lax.broadcasted_iota(
        jnp.int32, shape, 1
    )
    for own, others, total in ((image_ref, text_ref, image_sum), (text_ref, image_ref, text_sum)):
        chance = 1.0 / (1.0 + decay(factor, logits(own, others)))
        total[...] = product(chance - matched.astype(jnp.float32), others)
    is_1 = core().astype(jnp.float32)

    def use(value):
        image_sum[...] += value * is_1
        text_sum[...] += value * (1.0 - is_1)

    add_all(factor, [(near_own, join(near, joined), use)])


def step_kernel(factor, units, sides, *refs):
    is_1 = core().astype(jnp.float32)
    parts = []
    for _, count in units:
        parts.append((refs[0], refs[1 : 1 + count]))
        refs = refs[1 + count :]
    totals = dict(zip(sides, refs))
    sums = dict(zip(sides, refs[len(sides) :]))
    joined = refs[2 * len(sides) :]
    touched = set()

    def add(side, value):
        sums[side][...] = (sums if side in touched else totals)[side][...] + value
        touched.add(side)

    def use(side, value):
        if side < 2:
            add(side, value)
        else:
            add(side - 2, value * (1.0 - is_1))
            add(3 - side, value * is_1)

    add_all(
        factor,
        [
            (own, join(visitors, scratch), functools.partial(use, side))
            for (side, _), (own, visitors), scratch in zip(units, parts, joined)
        ],
    )


def last_kernel(factor, counts, far_own, far, *refs):
    parts = []
    for count in counts:
        parts.append((refs[0], refs[1 : 1 + count], refs[1 + count]))
        refs = refs[2 + count :]
    outs, helds, joined, sems = refs[:2], refs[2:4], refs[4:6], refs[6]
    starts = range(0, far_own.shape[0], LAST_TILE)
    is_1 = core().astype(jnp.float32)
    copies = []

    def use_far(start, value):
        rows = pl.ds(start, LAST_TILE)
        helds[0][rows] = parts[0][2][rows] + value * (1.0 - is_1)
        helds[1][rows] = parts[1][2][rows] + value * is_1

    def use(held, out, start, value):
        rows = pl.ds(start, LAST_TILE)
        held[rows] = (held[rows] + value) * factor
        for first in range(start, start + LAST_TILE, COPY_ROWS):
            span = pl.ds(first, COPY_ROWS)
            copies.append(pltpu.make_async_copy(held.at[span], out.at[span], sems.at[len(copies)]))
            copies[-1].start()

    def unit(own, others, start, act, *args):
        return (own.at[pl.ds(start, LAST_TILE)], others, functools.partial(act, *args, start))

    units = [unit(far_own, far, start, use_far) for start in starts]
    for (own, visitors, _), held, out, scratch in zip(parts, helds, outs, joined):
        others = join(visitors, scratch)
        units += [unit(own, others, start, use, held, out) for start in starts]
    add_all(factor, units)
    for copy in copies:
        copy.wait()


def local(image_embed, text_embed):
    rows, width = image_embed.shape
    dtype = image_embed.dtype
    factor = 2.0 / math.sqrt(width)
    kept = pltpu.VMEM((rows, width), jnp.float32)
    block = pltpu.VMEM((rows, width), dtype)
    grad = jax.ShapeDtypeStruct((rows, width), jnp.float32)

    def call(kernel, outs, operands, scratch=(), aliases=None, in_spec=VMEM):
        return pl.pallas_call(
            kernel,
            out_shape=tuple(outs),
            in_specs=[in_spec] * len(operands),
            out_specs=(ANY if outs[0] is grad else VMEM,) * len(outs),
            scratch_shapes=list(scratch),
            input_output_aliases=aliases or {},
            cost_estimate=pl.CostEstimate(flops=1, bytes_accessed=1, transcendentals=0),
            compiler_params=pltpu.CompilerParams(vmem_limit_bytes=VMEM_MIB << 20),
        )(*operands)

    def depth(visitors):
        return pltpu.VMEM((sum(visitor.shape[0] for visitor in visitors), width), dtype)

    def step(units, sums):
        sides = tuple(sums)
        operands = [ref for _, own, visitors in units for ref in (own, *visitors)]
        counts = [(side, len(visitors)) for side, _, visitors in units]
        return dict(
            zip(
                sides,
                call(
                    functools.partial(step_kernel, factor, counts, sides),
                    [kept] * len(sides),
                    (*operands, *sums.values()),
                    [depth(visitors) for _, _, visitors in units],
                    {len(operands) + k: k for k in range(len(sides))},
                ),
            )
        )

    def after(value, *earlier):
        return lax.optimization_barrier((value, *earlier))[0]

    def next_images(piece):
        return send(piece, lambda i: i - 2)

    def next_texts(piece):
        return send(piece, lambda i: i + 2)

    in_hbm = [pltpu.with_memory_space_constraint(x, pltpu.HBM) for x in (image_embed, text_embed)]
    images, texts = next_images(image_embed), next_texts(text_embed)
    far_own, near_own = call(
        core_pick_kernel, [block, block], in_hbm, [pltpu.SemaphoreType.DMA((2,))], in_spec=ANY
    )
    far = send(far_own, lambda i: i + 3 if i % 2 else i - 3)
    near = swap(near_own, 2)
    sums = call(
        functools.partial(own_kernel, factor),
        (kept, kept),
        (image_embed, text_embed, near_own, *near),
        [block],
    )
    sums = dict(enumerate(sums))

    images, texts = after(images, *sums.values()), after(texts, *sums.values())
    swapped_images, swapped_texts = swap(images, 1), swap(texts, 1)
    sums = step([(1, text_embed, (images,)), (0, image_embed, (texts,))], sums)
    operands = (image_embed, *swapped_texts, sums[0], text_embed, *swapped_images, sums[1])
    operands = (far_own, far, *operands)
    return call(
        functools.partial(last_kernel, factor, (1, 1)),
        (grad, grad),
        operands,
        [kept, kept, depth((texts,)), depth((images,))]
        + [pltpu.SemaphoreType.DMA((2 * rows // COPY_ROWS,))],
    )


def solution(mesh):
    spec = P(("rep", "blk"), None)
    return jax.shard_map(
        local, mesh=mesh, in_specs=(spec, spec), out_specs=(spec, spec), check_vma=False
    )
```

```python
import functools
import math

import jax
import jax.numpy as jnp
from jax import lax
from jax.experimental import pallas as pl
from jax.experimental.pallas import tpu as pltpu
from jax.sharding import PartitionSpec as P

AXIS = "blk"
NEAR_PARTS = 2
LAST_TILE = 256
COPY_ROWS = 128
VMEM_MIB = 32
VMEM = pl.BlockSpec(memory_space=pltpu.VMEM)
ANY = pl.BlockSpec(memory_space=pl.ANY)
LOG2_E = math.log2(math.e)


def send(block, target):
    count = lax.axis_size(AXIS)
    return lax.ppermute(block, AXIS, [(i, target(i) % count) for i in range(count)])


def swap(block, parts):
    return [send(part, lambda i: i ^ 1) for part in jnp.split(block, parts)]


def core():
    return lax.rem(lax.axis_index(AXIS), 2)


def logits(own, others):
    return lax.dot_general(
        own[...], others[...], (((1,), (1,)), ((), ())), preferred_element_type=jnp.float32
    )


def decay(factor, inner_prod):
    return jnp.exp2(LOG2_E - (factor * LOG2_E) * inner_prod)


def product(weight, others):
    return jnp.dot(weight.astype(jnp.bfloat16), others[...], preferred_element_type=jnp.float32)


def add_all(factor, units):
    following = logits(*units[0][:2])
    for k, (_, others, use) in enumerate(units):
        inner_prod = following
        if k + 1 < len(units):
            following = logits(*units[k + 1][:2])
        weight = pl.reciprocal(1.0 + decay(factor, inner_prod), approx=True)
        use(product(weight, others))


def join(visitors, joined):
    if len(visitors) == 1:
        return visitors[0]
    start = 0
    for visitor in visitors:
        joined[pl.ds(start, visitor.shape[0])] = visitor[...]
        start += visitor.shape[0]
    return joined.at[pl.ds(0, start)]


def core_pick_kernel(image_ref, text_ref, far_own, near_own, sems):
    for is_core, (far, near) in enumerate(((image_ref, text_ref), (text_ref, image_ref))):

        @pl.when(core() == is_core)
        def _():
            copies = [
                pltpu.make_async_copy(far, far_own, sems.at[0]),
                pltpu.make_async_copy(near, near_own, sems.at[1]),
            ]
            for copy in copies:
                copy.start()
            for copy in copies:
                copy.wait()


def own_kernel(factor, image_ref, text_ref, near_own, *refs):
    near, (image_sum, text_sum, joined) = refs[:NEAR_PARTS], refs[NEAR_PARTS:]
    rows = image_ref.shape[0]
    shape = (rows, rows)
    matched = lax.broadcasted_iota(jnp.int32, shape, 0) == lax.broadcasted_iota(
        jnp.int32, shape, 1
    )
    for own, others, total in ((image_ref, text_ref, image_sum), (text_ref, image_ref, text_sum)):
        chance = 1.0 / (1.0 + decay(factor, logits(own, others)))
        total[...] = product(chance - matched.astype(jnp.float32), others)
    is_1 = core().astype(jnp.float32)

    def use(value):
        image_sum[...] += value * is_1
        text_sum[...] += value * (1.0 - is_1)

    add_all(factor, [(near_own, join(near, joined), use)])


def step_kernel(factor, units, sides, *refs):
    is_1 = core().astype(jnp.float32)
    parts = []
    for _, count in units:
        parts.append((refs[0], refs[1 : 1 + count]))
        refs = refs[1 + count :]
    totals = dict(zip(sides, refs))
    sums = dict(zip(sides, refs[len(sides) :]))
    joined = refs[2 * len(sides) :]
    touched = set()

    def add(side, value):
        sums[side][...] = (sums if side in touched else totals)[side][...] + value
        touched.add(side)

    def use(side, value):
        if side < 2:
            add(side, value)
        else:
            add(side - 2, value * (1.0 - is_1))
            add(3 - side, value * is_1)

    add_all(
        factor,
        [
            (own, join(visitors, scratch), functools.partial(use, side))
            for (side, _), (own, visitors), scratch in zip(units, parts, joined)
        ],
    )


def last_kernel(factor, counts, far_own, far, *refs):
    parts = []
    for count in counts:
        parts.append((refs[0], refs[1 : 1 + count], refs[1 + count]))
        refs = refs[2 + count :]
    outs, helds, joined, sems = refs[:2], refs[2:4], refs[4:6], refs[6]
    starts = range(0, far_own.shape[0], LAST_TILE)
    is_1 = core().astype(jnp.float32)
    copies = []

    def use_far(start, value):
        rows = pl.ds(start, LAST_TILE)
        helds[0][rows] = parts[0][2][rows] + value * (1.0 - is_1)
        helds[1][rows] = parts[1][2][rows] + value * is_1

    def use(held, out, start, value):
        rows = pl.ds(start, LAST_TILE)
        held[rows] = (held[rows] + value) * factor
        for first in range(start, start + LAST_TILE, COPY_ROWS):
            span = pl.ds(first, COPY_ROWS)
            copies.append(pltpu.make_async_copy(held.at[span], out.at[span], sems.at[len(copies)]))
            copies[-1].start()

    def unit(own, others, start, act, *args):
        return (own.at[pl.ds(start, LAST_TILE)], others, functools.partial(act, *args, start))

    units = [unit(far_own, far, start, use_far) for start in starts]
    for (own, visitors, _), held, out, scratch in zip(parts, helds, outs, joined):
        others = join(visitors, scratch)
        units += [unit(own, others, start, use, held, out) for start in starts]
    add_all(factor, units)
    for copy in copies:
        copy.wait()


def local(image_embed, text_embed):
    rows, width = image_embed.shape
    dtype = image_embed.dtype
    factor = 2.0 / math.sqrt(width)
    kept = pltpu.VMEM((rows, width), jnp.float32)
    block = pltpu.VMEM((rows, width), dtype)
    grad = jax.ShapeDtypeStruct((rows, width), jnp.float32)

    def call(kernel, outs, operands, scratch=(), aliases=None, in_spec=VMEM):
        return pl.pallas_call(
            kernel,
            out_shape=tuple(outs),
            in_specs=[in_spec] * len(operands),
            out_specs=(ANY if outs[0] is grad else VMEM,) * len(outs),
            scratch_shapes=list(scratch),
            input_output_aliases=aliases or {},
            cost_estimate=pl.CostEstimate(flops=1, bytes_accessed=1, transcendentals=0),
            compiler_params=pltpu.CompilerParams(vmem_limit_bytes=VMEM_MIB << 20),
        )(*operands)

    def depth(visitors):
        return pltpu.VMEM((sum(visitor.shape[0] for visitor in visitors), width), dtype)

    def step(units, sums):
        sides = tuple(sums)
        operands = [ref for _, own, visitors in units for ref in (own, *visitors)]
        counts = [(side, len(visitors)) for side, _, visitors in units]
        return dict(
            zip(
                sides,
                call(
                    functools.partial(step_kernel, factor, counts, sides),
                    [kept] * len(sides),
                    (*operands, *sums.values()),
                    [depth(visitors) for _, _, visitors in units],
                    {len(operands) + k: k for k in range(len(sides))},
                ),
            )
        )

    def after(value, *earlier):
        return lax.optimization_barrier((value, *earlier))[0]

    def next_images(piece):
        return send(piece, lambda i: i - 2)

    def next_texts(piece):
        return send(piece, lambda i: i + 2)

    in_hbm = [pltpu.with_memory_space_constraint(x, pltpu.HBM) for x in (image_embed, text_embed)]
    images, texts = next_images(image_embed), next_texts(text_embed)
    far_own, near_own = call(
        core_pick_kernel, [block, block], in_hbm, [pltpu.SemaphoreType.DMA((2,))], in_spec=ANY
    )
    far = send(far_own, lambda i: i + 3 if i % 2 else i - 3)
    near = swap(near_own, 2)
    sums = call(
        functools.partial(own_kernel, factor),
        (kept, kept),
        (image_embed, text_embed, near_own, *near),
        [block],
    )
    sums = dict(enumerate(sums))

    images, texts = after(images, *sums.values()), after(texts, *sums.values())
    swapped_images, swapped_texts = swap(images, 1), swap(texts, 2)
    sums = step([(1, text_embed, (images,)), (0, image_embed, (texts,))], sums)
    operands = (image_embed, *swapped_texts, sums[0], text_embed, *swapped_images, sums[1])
    operands = (far_own, far, *operands)
    return call(
        functools.partial(last_kernel, factor, (2, 1)),
        (grad, grad),
        operands,
        [kept, kept, depth((texts,)), depth((images,))]
        + [pltpu.SemaphoreType.DMA((2 * rows // COPY_ROWS,))],
    )


def solution(mesh):
    spec = P(("rep", "blk"), None)
    return jax.shard_map(
        local, mesh=mesh, in_specs=(spec, spec), out_specs=(spec, spec), check_vma=False
    )
```

```python
import functools
import math

import jax
import jax.numpy as jnp
from jax import lax
from jax.experimental import pallas as pl
from jax.experimental.pallas import tpu as pltpu
from jax.sharding import PartitionSpec as P

AXIS = "blk"
NEAR_PARTS = 2
LAST_TILE = 256
COPY_ROWS = 128
VMEM_MIB = 32
VMEM = pl.BlockSpec(memory_space=pltpu.VMEM)
ANY = pl.BlockSpec(memory_space=pl.ANY)
LOG2_E = math.log2(math.e)


def send(block, target):
    count = lax.axis_size(AXIS)
    return lax.ppermute(block, AXIS, [(i, target(i) % count) for i in range(count)])


def swap(block, parts):
    return [send(part, lambda i: i ^ 1) for part in jnp.split(block, parts)]


def core():
    return lax.rem(lax.axis_index(AXIS), 2)


def logits(own, others):
    return lax.dot_general(
        own[...], others[...], (((1,), (1,)), ((), ())), preferred_element_type=jnp.float32
    )


def decay(factor, inner_prod):
    return jnp.exp2(LOG2_E - (factor * LOG2_E) * inner_prod)


def product(weight, others):
    return jnp.dot(weight.astype(jnp.bfloat16), others[...], preferred_element_type=jnp.float32)


def add_all(factor, units):
    following = logits(*units[0][:2])
    for k, (_, others, use) in enumerate(units):
        inner_prod = following
        if k + 1 < len(units):
            following = logits(*units[k + 1][:2])
        weight = pl.reciprocal(1.0 + decay(factor, inner_prod), approx=True)
        use(product(weight, others))


def join(visitors, joined):
    if len(visitors) == 1:
        return visitors[0]
    start = 0
    for visitor in visitors:
        joined[pl.ds(start, visitor.shape[0])] = visitor[...]
        start += visitor.shape[0]
    return joined.at[pl.ds(0, start)]


def core_pick_kernel(image_ref, text_ref, far_own, near_own, sems):
    for is_core, (far, near) in enumerate(((image_ref, text_ref), (text_ref, image_ref))):

        @pl.when(core() == is_core)
        def _():
            copies = [
                pltpu.make_async_copy(far, far_own, sems.at[0]),
                pltpu.make_async_copy(near, near_own, sems.at[1]),
            ]
            for copy in copies:
                copy.start()
            for copy in copies:
                copy.wait()


def own_kernel(factor, image_ref, text_ref, near_own, *refs):
    near, (image_sum, text_sum, joined) = refs[:NEAR_PARTS], refs[NEAR_PARTS:]
    rows = image_ref.shape[0]
    shape = (rows, rows)
    matched = lax.broadcasted_iota(jnp.int32, shape, 0) == lax.broadcasted_iota(
        jnp.int32, shape, 1
    )
    for own, others, total in ((image_ref, text_ref, image_sum), (text_ref, image_ref, text_sum)):
        chance = 1.0 / (1.0 + decay(factor, logits(own, others)))
        total[...] = product(chance - matched.astype(jnp.float32), others)
    is_1 = core().astype(jnp.float32)

    def use(value):
        image_sum[...] += value * is_1
        text_sum[...] += value * (1.0 - is_1)

    add_all(factor, [(near_own, join(near, joined), use)])


def step_kernel(factor, units, sides, *refs):
    is_1 = core().astype(jnp.float32)
    parts = []
    for _, count in units:
        parts.append((refs[0], refs[1 : 1 + count]))
        refs = refs[1 + count :]
    totals = dict(zip(sides, refs))
    sums = dict(zip(sides, refs[len(sides) :]))
    joined = refs[2 * len(sides) :]
    touched = set()

    def add(side, value):
        sums[side][...] = (sums if side in touched else totals)[side][...] + value
        touched.add(side)

    def use(side, value):
        if side < 2:
            add(side, value)
        else:
            add(side - 2, value * (1.0 - is_1))
            add(3 - side, value * is_1)

    add_all(
        factor,
        [
            (own, join(visitors, scratch), functools.partial(use, side))
            for (side, _), (own, visitors), scratch in zip(units, parts, joined)
        ],
    )


def last_kernel(factor, counts, far_own, far, *refs):
    parts = []
    for count in counts:
        parts.append((refs[0], refs[1 : 1 + count], refs[1 + count]))
        refs = refs[2 + count :]
    outs, helds, joined, far_held, sems = refs[:2], refs[2:4], refs[4:6], refs[6], refs[7]
    starts = range(0, far_own.shape[0], LAST_TILE)
    is_1 = core().astype(jnp.float32)
    masks = ((1.0 - is_1) * factor, is_1 * factor)
    copies = []

    def use_far(start, value):
        far_held[pl.ds(start, LAST_TILE)] = value

    def use(side, start, value):
        rows = pl.ds(start, LAST_TILE)
        held, out = helds[side], outs[side]
        held[rows] = (parts[side][2][rows] + value) * factor + far_held[rows] * masks[side]
        for first in range(start, start + LAST_TILE, COPY_ROWS):
            span = pl.ds(first, COPY_ROWS)
            copies.append(pltpu.make_async_copy(held.at[span], out.at[span], sems.at[len(copies)]))
            copies[-1].start()

    def unit(own, others, start, act, *args):
        return (own.at[pl.ds(start, LAST_TILE)], others, functools.partial(act, *args, start))

    units = [unit(far_own, far, start, use_far) for start in starts]
    for side, ((own, visitors, _), scratch) in enumerate(zip(parts, joined)):
        others = join(visitors, scratch)
        units += [unit(own, others, start, use, side) for start in starts]
    add_all(factor, units)
    for copy in copies:
        copy.wait()


def local(image_embed, text_embed):
    rows, width = image_embed.shape
    dtype = image_embed.dtype
    factor = 2.0 / math.sqrt(width)
    kept = pltpu.VMEM((rows, width), jnp.float32)
    block = pltpu.VMEM((rows, width), dtype)
    grad = jax.ShapeDtypeStruct((rows, width), jnp.float32)

    def call(kernel, outs, operands, scratch=(), aliases=None, in_spec=VMEM):
        return pl.pallas_call(
            kernel,
            out_shape=tuple(outs),
            in_specs=[in_spec] * len(operands),
            out_specs=(ANY if outs[0] is grad else VMEM,) * len(outs),
            scratch_shapes=list(scratch),
            input_output_aliases=aliases or {},
            cost_estimate=pl.CostEstimate(flops=1, bytes_accessed=1, transcendentals=0),
            compiler_params=pltpu.CompilerParams(vmem_limit_bytes=VMEM_MIB << 20),
        )(*operands)

    def depth(visitors):
        return pltpu.VMEM((sum(visitor.shape[0] for visitor in visitors), width), dtype)

    def step(units, sums):
        sides = tuple(sums)
        operands = [ref for _, own, visitors in units for ref in (own, *visitors)]
        counts = [(side, len(visitors)) for side, _, visitors in units]
        return dict(
            zip(
                sides,
                call(
                    functools.partial(step_kernel, factor, counts, sides),
                    [kept] * len(sides),
                    (*operands, *sums.values()),
                    [depth(visitors) for _, _, visitors in units],
                    {len(operands) + k: k for k in range(len(sides))},
                ),
            )
        )

    def after(value, *earlier):
        return lax.optimization_barrier((value, *earlier))[0]

    def next_images(piece):
        return send(piece, lambda i: i - 2)

    def next_texts(piece):
        return send(piece, lambda i: i + 2)

    in_hbm = [pltpu.with_memory_space_constraint(x, pltpu.HBM) for x in (image_embed, text_embed)]
    images, texts = next_images(image_embed), next_texts(text_embed)
    far_own, near_own = call(
        core_pick_kernel, [block, block], in_hbm, [pltpu.SemaphoreType.DMA((2,))], in_spec=ANY
    )
    far = send(far_own, lambda i: i + 3 if i % 2 else i - 3)
    near = swap(near_own, 2)
    sums = call(
        functools.partial(own_kernel, factor),
        (kept, kept),
        (image_embed, text_embed, near_own, *near),
        [block],
    )
    sums = dict(enumerate(sums))

    images, texts = after(images, *sums.values()), after(texts, *sums.values())
    swapped_images, swapped_texts = swap(images, 1), swap(texts, 2)
    sums = step([(1, text_embed, (images,)), (0, image_embed, (texts,))], sums)
    operands = (image_embed, *swapped_texts, sums[0], text_embed, *swapped_images, sums[1])
    operands = (far_own, far, *operands)
    return call(
        functools.partial(last_kernel, factor, (2, 1)),
        (grad, grad),
        operands,
        [kept, kept, depth((texts,)), depth((images,))]
        + [kept, pltpu.SemaphoreType.DMA((2 * rows // COPY_ROWS,))],
    )


def solution(mesh):
    spec = P(("rep", "blk"), None)
    return jax.shard_map(
        local, mesh=mesh, in_specs=(spec, spec), out_specs=(spec, spec), check_vma=False
    )
```

```python
import functools
import math

import jax
import jax.numpy as jnp
from jax import lax
from jax.experimental import pallas as pl
from jax.experimental.pallas import tpu as pltpu
from jax.sharding import PartitionSpec as P

AXIS = "blk"
NEAR_PARTS = 2
LAST_TILE = 256
COPY_ROWS = 128
VMEM_MIB = 32
VMEM = pl.BlockSpec(memory_space=pltpu.VMEM)
ANY = pl.BlockSpec(memory_space=pl.ANY)
LOG2_E = math.log2(math.e)


def send(block, target):
    count = lax.axis_size(AXIS)
    return lax.ppermute(block, AXIS, [(i, target(i) % count) for i in range(count)])


def swap(block, parts):
    return [send(part, lambda i: i ^ 1) for part in jnp.split(block, parts)]


def core():
    return lax.rem(lax.axis_index(AXIS), 2)


def logits(own, others):
    return lax.dot_general(
        own[...], others[...], (((1,), (1,)), ((), ())), preferred_element_type=jnp.float32
    )


def decay(factor, inner_prod):
    return jnp.exp2(LOG2_E - (factor * LOG2_E) * inner_prod)


def product(weight, others):
    return jnp.dot(weight.astype(jnp.bfloat16), others[...], preferred_element_type=jnp.float32)


def add_all(factor, units):
    following = logits(*units[0][:2])
    for k, (_, others, use) in enumerate(units):
        inner_prod = following
        if k + 1 < len(units):
            following = logits(*units[k + 1][:2])
        weight = pl.reciprocal(1.0 + decay(factor, inner_prod), approx=True)
        use(product(weight, others))


def join(visitors, joined):
    if len(visitors) == 1:
        return visitors[0]
    start = 0
    for visitor in visitors:
        joined[pl.ds(start, visitor.shape[0])] = visitor[...]
        start += visitor.shape[0]
    return joined.at[pl.ds(0, start)]


def core_pick_kernel(image_ref, text_ref, far_own, near_own, sems):
    for is_core, (far, near) in enumerate(((image_ref, text_ref), (text_ref, image_ref))):

        @pl.when(core() == is_core)
        def _():
            copies = [
                pltpu.make_async_copy(far, far_own, sems.at[0]),
                pltpu.make_async_copy(near, near_own, sems.at[1]),
            ]
            for copy in copies:
                copy.start()
            for copy in copies:
                copy.wait()


def own_kernel(factor, image_ref, text_ref, near_own, *refs):
    near, (image_sum, text_sum, joined) = refs[:NEAR_PARTS], refs[NEAR_PARTS:]
    rows = image_ref.shape[0]
    shape = (rows, rows)
    matched = lax.broadcasted_iota(jnp.int32, shape, 0) == lax.broadcasted_iota(
        jnp.int32, shape, 1
    )
    for own, others, total in ((image_ref, text_ref, image_sum), (text_ref, image_ref, text_sum)):
        chance = 1.0 / (1.0 + decay(factor, logits(own, others)))
        total[...] = product(chance - matched.astype(jnp.float32), others)
    is_1 = core().astype(jnp.float32)

    def use(value):
        image_sum[...] += value * is_1
        text_sum[...] += value * (1.0 - is_1)

    add_all(factor, [(near_own, join(near, joined), use)])


def step_kernel(factor, units, sides, *refs):
    is_1 = core().astype(jnp.float32)
    parts = []
    for _, count in units:
        parts.append((refs[0], refs[1 : 1 + count]))
        refs = refs[1 + count :]
    totals = dict(zip(sides, refs))
    sums = dict(zip(sides, refs[len(sides) :]))
    joined = refs[2 * len(sides) :]
    touched = set()

    def add(side, value):
        sums[side][...] = (sums if side in touched else totals)[side][...] + value
        touched.add(side)

    def use(side, value):
        if side < 2:
            add(side, value)
        else:
            add(side - 2, value * (1.0 - is_1))
            add(3 - side, value * is_1)

    add_all(
        factor,
        [
            (own, join(visitors, scratch), functools.partial(use, side))
            for (side, _), (own, visitors), scratch in zip(units, parts, joined)
        ],
    )


def last_kernel(factor, counts, far_own, far, *refs):
    parts = []
    for count in counts:
        parts.append((refs[0], refs[1 : 1 + count], refs[1 + count]))
        refs = refs[2 + count :]
    outs, helds, joined, far_held, sems = refs[:2], refs[2:4], refs[4:6], refs[6], refs[7]
    starts = range(0, far_own.shape[0], LAST_TILE)
    is_1 = core().astype(jnp.float32)
    masks = ((1.0 - is_1) * factor, is_1 * factor)
    copies = []

    def use_far(start, value):
        far_held[pl.ds(start, LAST_TILE)] = value

    def use(side, start, value):
        rows = pl.ds(start, LAST_TILE)
        held, out = helds[side], outs[side]
        held[rows] = (parts[side][2][rows] + value) * factor + far_held[rows] * masks[side]
        for first in range(start, start + LAST_TILE, COPY_ROWS):
            span = pl.ds(first, COPY_ROWS)
            copies.append(pltpu.make_async_copy(held.at[span], out.at[span], sems.at[len(copies)]))
            copies[-1].start()

    def unit(own, others, start, act, *args):
        return (own.at[pl.ds(start, LAST_TILE)], others, functools.partial(act, *args, start))

    met = [join(visitors, scratch) for (_, visitors, _), scratch in zip(parts, joined)]
    units = []
    for start in starts:
        units.append(unit(far_own, far, start, use_far))
        for side in (0, 1):
            units.append(unit(parts[side][0], met[side], start, use, side))
    add_all(factor, units)
    for copy in copies:
        copy.wait()


def local(image_embed, text_embed):
    rows, width = image_embed.shape
    dtype = image_embed.dtype
    factor = 2.0 / math.sqrt(width)
    kept = pltpu.VMEM((rows, width), jnp.float32)
    block = pltpu.VMEM((rows, width), dtype)
    grad = jax.ShapeDtypeStruct((rows, width), jnp.float32)

    def call(kernel, outs, operands, scratch=(), aliases=None, in_spec=VMEM):
        return pl.pallas_call(
            kernel,
            out_shape=tuple(outs),
            in_specs=[in_spec] * len(operands),
            out_specs=(ANY if outs[0] is grad else VMEM,) * len(outs),
            scratch_shapes=list(scratch),
            input_output_aliases=aliases or {},
            cost_estimate=pl.CostEstimate(flops=1, bytes_accessed=1, transcendentals=0),
            compiler_params=pltpu.CompilerParams(vmem_limit_bytes=VMEM_MIB << 20),
        )(*operands)

    def depth(visitors):
        return pltpu.VMEM((sum(visitor.shape[0] for visitor in visitors), width), dtype)

    def step(units, sums):
        sides = tuple(sums)
        operands = [ref for _, own, visitors in units for ref in (own, *visitors)]
        counts = [(side, len(visitors)) for side, _, visitors in units]
        return dict(
            zip(
                sides,
                call(
                    functools.partial(step_kernel, factor, counts, sides),
                    [kept] * len(sides),
                    (*operands, *sums.values()),
                    [depth(visitors) for _, _, visitors in units],
                    {len(operands) + k: k for k in range(len(sides))},
                ),
            )
        )

    def after(value, *earlier):
        return lax.optimization_barrier((value, *earlier))[0]

    def next_images(piece):
        return send(piece, lambda i: i - 2)

    def next_texts(piece):
        return send(piece, lambda i: i + 2)

    in_hbm = [pltpu.with_memory_space_constraint(x, pltpu.HBM) for x in (image_embed, text_embed)]
    images, texts = next_images(image_embed), next_texts(text_embed)
    far_own, near_own = call(
        core_pick_kernel, [block, block], in_hbm, [pltpu.SemaphoreType.DMA((2,))], in_spec=ANY
    )
    far = send(far_own, lambda i: i + 3 if i % 2 else i - 3)
    near = swap(near_own, 2)
    sums = call(
        functools.partial(own_kernel, factor),
        (kept, kept),
        (image_embed, text_embed, near_own, *near),
        [block],
    )
    sums = dict(enumerate(sums))

    images, texts = after(images, *sums.values()), after(texts, *sums.values())
    swapped_images, swapped_texts = swap(images, 1), swap(texts, 2)
    sums = step([(1, text_embed, (images,)), (0, image_embed, (texts,))], sums)
    operands = (image_embed, *swapped_texts, sums[0], text_embed, *swapped_images, sums[1])
    operands = (far_own, far, *operands)
    return call(
        functools.partial(last_kernel, factor, (2, 1)),
        (grad, grad),
        operands,
        [kept, kept, depth((texts,)), depth((images,))]
        + [kept, pltpu.SemaphoreType.DMA((2 * rows // COPY_ROWS,))],
    )


def solution(mesh):
    spec = P(("rep", "blk"), None)
    return jax.shard_map(
        local, mesh=mesh, in_specs=(spec, spec), out_specs=(spec, spec), check_vma=False
    )
```
